768 devices in a mesh: gx: 12 (over z), gy: 4 (over x), gz: 16 (over y, core).
Axes of the slice: x: 4, y: 8, z: 12, core: 2. Of those that a mesh axis runs over, the one named last changes fastest.
Arguments:
- right_side: float32 [288, 128, 1024], P('gx', 'gz', 'gy'), may hold values from -40 to 40
- kappa: float32 [288, 128, 1024], P('gx', 'gz', 'gy'), may hold values from 0.5 to 4
Outputs:
- solution: float32 [288, 128, 1024], P('gx', 'gz', 'gy')
- residual: float32 [288, 128, 1024], P('gx', 'gz', 'gy')
- res_image: float32 [288, 128, 1024], P('gx', 'gz', 'gy')
- direction: float32 [288, 128, 1024], P('gx', 'gz', 'gy')
The draws below stay inside these ranges and needn't reach their ends.
All inputs are finite; a program needn't handle non-finite values.
Results may differ from the reference program's by a relative error of at most 0.00025.
Values sent between devices are 32-bit elements; how exact they have to be, the bound alone decides.
A program may use at most 32 MiB of HBM per device.

```python
import math
import jax
import jax.numpy as jnp

ITERS = 4
NX = 288
NZ = 128
NY = 1024


def draw_right_side(key, part):
    key = jax.random.fold_in(key, 11)
    pos_x = jnp.arange(NX, dtype=jnp.float32) / (NX - 1)
    pos_z = jnp.arange(NZ, dtype=jnp.float32) / (NZ - 1)
    pos_y = jnp.arange(NY, dtype=jnp.float32) / (NY - 1)
    scale = jnp.exp(jnp.log(3.0) * (pos_x[:, None, None] + pos_z[None, :, None] + pos_y[None, None, :])) / 9.0
    values = jnp.clip(jax.random.normal(key, (NX, NZ, NY), jnp.float32), -4.0, 4.0) * scale
    return jnp.clip(values, -40.0, 40.0).astype(jnp.float32)


def block_levels(own_key, shape, shards, low, top_value):
    level, own = 1.0, jax.random.fold_in(own_key, 6)
    for axis_at, parts in shards:
        draws = jnp.exp(jax.random.uniform(jax.random.fold_in(own, axis_at), (parts,), jnp.float32, low / len(shards), top_value / len(shards)))
        level = level * jnp.repeat(draws, shape[axis_at] // parts).reshape([-1 if axis == axis_at else 1 for axis in range(len(shape))])
    return level


def setup_inputs(seed: int = 0) -> dict:
    splits = jax.random.split(jax.random.key(seed), 3)
    right_side = draw_right_side(jax.random.fold_in(splits[2], 71), 0)
    kappa = jnp.clip(jnp.exp(math.log(4.0) - 2.0794415 * jax.random.uniform(splits[1], (NX, NZ, NY), jnp.float32) ** block_levels(splits[1], (NX, NZ, NY), ((0, 12), (1, 16), (2, 4)), -0.2, 0.2)), 0.5, 4.0)
    return {"right_side": right_side, "kappa": kappa}


def conductances(kappa):
    padded = jnp.pad(kappa, 1)
    centre = padded[1:-1, 1:-1, 1:-1]
    return (
        (centre + padded[2:, 1:-1, 1:-1]) * 0.5,
        (centre + padded[:-2, 1:-1, 1:-1]) * 0.5,
        (centre + padded[1:-1, 2:, 1:-1]) * 0.5,
        (centre + padded[1:-1, :-2, 1:-1]) * 0.5,
        (centre + padded[1:-1, 1:-1, 2:]) * 0.5,
        (centre + padded[1:-1, 1:-1, :-2]) * 0.5,
    )


def operate(field, conds):
    padded = jnp.pad(field, 1)
    total = conds[0] * (field - padded[2:, 1:-1, 1:-1])
    total = total + conds[1] * (field - padded[:-2, 1:-1, 1:-1])
    total = total + conds[2] * (field - padded[1:-1, 2:, 1:-1])
    total = total + conds[3] * (field - padded[1:-1, :-2, 1:-1])
    total = total + conds[4] * (field - padded[1:-1, 1:-1, 2:])
    total = total + conds[5] * (field - padded[1:-1, 1:-1, :-2])
    return total


def reference(right_side, kappa):
    conds = conductances(kappa)
    solution = jnp.zeros_like(right_side)
    residual = right_side
    res_image = operate(residual, conds)
    direction = jnp.zeros_like(right_side)
    dir_image = jnp.zeros_like(right_side)
    dir_square = jnp.zeros_like(right_side)
    prior_norm = jnp.float32(1.0)
    prior_step = jnp.float32(1.0)
    for turn in range(ITERS):
        norm_now = jnp.sum(residual * residual)
        inner = jnp.sum(res_image * residual)
        fresh = operate(res_image, conds)
        if turn == 0:
            ratio = jnp.zeros_like(norm_now)
            step_len = norm_now / inner
        else:
            ratio = norm_now / prior_norm
            step_len = norm_now / (inner - ratio * norm_now / prior_step)
        dir_square = fresh + ratio * dir_square
        dir_image = res_image + ratio * dir_image
        direction = residual + ratio * direction
        solution = solution + step_len * direction
        residual = residual - step_len * dir_image
        res_image = res_image - step_len * dir_square
        prior_norm = norm_now
        prior_step = step_len
    return solution, residual, res_image, direction
```

```python
import functools

import jax
import jax.numpy as jnp
from jax import lax
from jax.experimental import pallas as pl
from jax.experimental.pallas import tpu as pltpu
from jax.sharding import PartitionSpec as P

MESH = pl.DeviceIdType.MESH
F32 = jnp.float32
NX, NZ, NY = 24, 8, 256
LANES = 128
GRAM = ((0, 1), (0, 2), (0, 3), (1, 1), (1, 2), (1, 3), (2, 2), (2, 3), (3, 3), (3, 4))


def shifted(axis, step):
    count = lax.axis_size(axis)
    return {axis: lax.rem(lax.axis_index(axis) + (step + count), count)}


def ring(step, count):
    return min(step % count, (-step) % count)


def group_line():
    lines = lax.axis_size("gx")
    gx, gz = lax.axis_index("gx"), lax.axis_index("gz")
    core = lax.rem(gz, 2)
    offsets = [(d, c) for d in range(lines) for c in range(2) if (d, c) != (0, 0)]
    offsets.sort(key=lambda o: -(2 * ring(o[0], lines) + o[1]))
    peers = [
        {"gx": lax.rem(gx + d, lines), "gz": gz - core + lax.rem(core + c, 2)} for d, c in offsets
    ]
    return gx * 2 + core, 2 * lines, peers


def group_plane():
    wide, deep = lax.axis_size("gy"), lax.axis_size("gz") // 2
    gy, gz = lax.axis_index("gy"), lax.axis_index("gz")
    offsets = [(d, e) for d in range(deep) for e in range(wide) if (d, e) != (0, 0)]
    offsets.sort(key=lambda o: -(ring(o[0], deep) + ring(o[1], wide)))
    peers = [
        {"gy": lax.rem(gy + e, wide), "gz": lax.rem(gz + 2 * d, 2 * deep)} for d, e in offsets
    ]
    return (gz // 2) * wide + gy, wide * deep, peers


def full(value):
    return jnp.broadcast_to(value, (NZ, LANES))


def total(value):
    return jnp.sum(jnp.sum(value, axis=0, keepdims=True), axis=1, keepdims=True)


def to_row(values):
    lane = lax.broadcasted_iota(jnp.int32, (1, LANES), 1)
    row = jnp.zeros((1, LANES), F32)
    for at, value in enumerate(values):
        row = jnp.where(lane == at, jnp.broadcast_to(total(value), (1, LANES)), row)
    return row


def solve(gram, c, s2):
    zero = jnp.zeros_like(c)
    one = jnp.ones_like(c)

    def g(i, j):
        return gram[(min(i, j), max(i, j))]

    gram = dict(gram)
    gram[(0, 4)] = g(1, 3) - s2 * g(0, 2)
    gram[(1, 4)] = g(2, 3) + s2 * (g(0, 3) - g(1, 2))
    gram[(2, 4)] = g(3, 3) + s2 * (g(1, 3) - g(2, 2))

    def image(a, top):
        out = []
        for i in range(top + 2):
            term = None
            if i <= top:
                term = c * a[i]
            if i >= 1:
                term = a[i - 1] if term is None else term + a[i - 1]
            if i + 1 <= top:
                term = term + s2 * a[i + 1]
            out.append(term)
        return out

    energy = {}
    for i in range(4):
        for j in range(i, 4):
            term = g(i, j + 1) + c * g(i, j)
            if j >= 1:
                term = term + s2 * g(i, j - 1)
            energy[(i, j)] = term

    def form(matrix, a, top):
        out = None
        for i in range(top + 1):
            part = matrix[(i, i)] * a[i]
            for j in range(i + 1, top + 1):
                part = part + (matrix[(i, j)] * 2.0) * a[j]
            out = a[i] * part if out is None else out + a[i] * part
        return out

    rho, way, answer = [one], [], []
    prior_norm = prior_step = None
    for turn in range(4):
        norm_now = form(gram, rho, turn)
        inner = form(energy, rho, turn)
        if turn == 0:
            step = norm_now / inner
            way = list(rho)
        else:
            ratio = norm_now / prior_norm
            step = norm_now / (inner - ratio * norm_now / prior_step)
            way = [rho[i] + ratio * way[i] if i < turn else rho[i] for i in range(turn + 1)]
        answer = [answer[i] + step * way[i] if i < turn else step * way[i] for i in range(turn + 1)]
        moved = image(way, turn)
        rho = [rho[i] - step * moved[i] if i <= turn else zero - step * moved[i] for i in range(turn + 2)]
        prior_norm, prior_step = norm_now, step
    third = image(rho[:4], 3)
    return answer, rho, third + [rho[4]], way


def main_kernel(b_hbm, k_hbm, w_hbm, coef_ref,
                V, K, W, CX, CZL, CZH, CYL, CYH, XS0, XR0, ZS, ZR, YS, YR, RS, RA, RB,
                copy_sem, out_sem, halo_send, halo_recv, red_send, red_recv):
    gx, gy, gz = lax.axis_index("gx"), lax.axis_index("gy"), lax.axis_index("gz")
    core = lax.rem(gz, 2)
    rank_a, count_a, peers_a = group_line()
    rank_b, count_b, peers_b = group_plane()
    across = {"gz": lax.rem(gz + 2 * core - 1 + lax.axis_size("gz"), lax.axis_size("gz"))}

    barrier = pltpu.get_barrier_semaphore()
    greeted = peers_b + peers_a + [across]
    for peer in greeted:
        pl.semaphore_signal(barrier, inc=1, device_id=peer, device_id_type=MESH)

    loads = []
    for half in (0, 1):
        at = slice(half * LANES, (half + 1) * LANES)
        loads.append(pltpu.make_async_copy(b_hbm.at[:, :, at], V.at[0, 1:NX + 1, half], copy_sem.at[0, half]))
        loads.append(pltpu.make_async_copy(k_hbm.at[:, :, at], K.at[1:NX + 1, half], copy_sem.at[1, half]))
    for load in loads:
        load.start()

    lane = lax.broadcasted_iota(jnp.int32, (NZ, LANES), 1)
    row = lax.broadcasted_iota(jnp.int32, (NZ, LANES), 0)
    inside = {
        ("gx", 0): gx > 0, ("gx", 1): gx < lax.axis_size("gx") - 1,
        ("gy", 0): gy > 0, ("gy", 1): gy < lax.axis_size("gy") - 1,
        ("gz", 0): gz > 0, ("gz", 1): gz < lax.axis_size("gz") - 1,
    }
    target = {
        (axis, slot): shifted(axis, 1 if slot == 0 else -1) for axis in ("gx", "gy", "gz") for slot in (0, 1)
    }
    order = [("gz", 0), ("gz", 1), ("gx", 0), ("gx", 1), ("gy", 0), ("gy", 1)]

    def copies(phase):
        out = {}
        for at, (axis, slot) in enumerate(order):
            if axis == "gx":
                if phase == 0:
                    src, dst = XS0.at[slot], XR0.at[slot]
                else:
                    src = V.at[phase, NX if slot == 0 else 1]
                    dst = V.at[phase, 0 if slot == 0 else NX + 1]
            elif axis == "gz":
                src, dst = ZS[min(phase, 1)], ZR[min(phase, 1)]
                src, dst = (src.at[slot], dst.at[slot]) if phase == 0 else (src.at[phase, slot], dst.at[phase, slot])
            else:
                src, dst = YS[min(phase, 1)], YR[min(phase, 1)]
                src, dst = (src.at[slot], dst.at[slot]) if phase == 0 else (src.at[phase, slot], dst.at[phase, slot])
            out[(axis, slot)] = pltpu.make_async_remote_copy(
                src_ref=src, dst_ref=dst, send_sem=halo_send.at[phase, at], recv_sem=halo_recv.at[phase, at],
                device_id=target[(axis, slot)], device_id_type=MESH,
            )
        return out

    def edge_rows(flat, dst, at):
        for half in (0, 1):
            dst[half] = flat[pl.ds(2 * NZ + half * NZ + at, NX, stride=2 * NZ), :]

    def start_halo(phase):
        flat = V.at[phase].reshape((NX + 2) * 2 * NZ, LANES)
        edge_rows(flat, ZS[1].at[phase, 0], NZ - 1)
        edge_rows(flat, ZS[1].at[phase, 1], 0)
        sent = copies(phase)
        for name in order:
            sent[name].start()
        return sent

    def keep(flag, value):
        return jnp.where(flag, value, jnp.zeros_like(value))

    def end_halo(phase, sent):
        for name in order:
            sent[name].wait_recv()
        V[phase, 0] = keep(inside[("gx", 0)], V[phase, 0])
        V[phase, NX + 1] = keep(inside[("gx", 1)], V[phase, NX + 1])
        for slot in (0, 1):
            ZR[1][phase, slot] = keep(inside[("gz", slot)], ZR[1][phase, slot])
        return [keep(inside[("gy", slot)], YR[1][phase, slot]) for slot in (0, 1)]

    def tiles(ref, *at):
        return ref[(*at, 0)], ref[(*at, 1)]

    def put(ref, at, pair):
        ref[(*at, 0)], ref[(*at, 1)] = pair

    def lanes_down(pair, packed, x):
        first, second = pltpu.roll(pair[0], 1, 1), pltpu.roll(pair[1], 1, 1)
        edge = pltpu.roll(packed, lax.rem(LANES - x, LANES), 1)
        return jnp.where(lane == 0, edge, first), jnp.where(lane == 0, first, second)

    def lanes_up(pair, packed, x):
        first, second = pltpu.roll(pair[0], LANES - 1, 1), pltpu.roll(pair[1], LANES - 1, 1)
        edge = pltpu.roll(packed, LANES - 1 - x, 1)
        return jnp.where(lane == LANES - 1, second, first), jnp.where(lane == LANES - 1, edge, second)

    def rows_down(pair, halo):
        return tuple(jnp.where(row == 0, full(h), pltpu.roll(p, 1, 0)) for p, h in zip(pair, halo))

    def rows_up(pair, halo):
        return tuple(jnp.where(row == NZ - 1, full(h), pltpu.roll(p, NZ - 1, 0)) for p, h in zip(pair, halo))

    def halo_row(ref, at, x):
        return tuple(ref[(*at, half, pl.ds(x, 1), slice(None))] for half in (0, 1))

    def pack_edges(pair, packed, x):
        up = jnp.where(lane == x, pltpu.roll(pair[1], lax.rem(x + 1, LANES), 1), packed[0])
        down = jnp.where(lane == x, pltpu.roll(pair[0], x, 1), packed[1])
        return up, down

    blank = jnp.zeros((NZ, LANES), F32)

    def loop(body, carry):
        return lax.fori_loop(0, NX, body, carry, unroll=True)

    for load in loads:
        load.wait()

    def pack_both(x, packed):
        field = pack_edges(tiles(V, 0, x + 1), packed[:2], x)
        coeff = pack_edges(tiles(K, x + 1), packed[2:], x)
        return field + coeff

    packed = loop(pack_both, (blank,) * 4)
    YS[0][0, 0], YS[0][1, 0], YS[0][0, 1], YS[0][1, 1] = packed
    flat_v = V.at[0].reshape((NX + 2) * 2 * NZ, LANES)
    flat_k = K.reshape((NX + 2) * 2 * NZ, LANES)
    for slot, at, x in ((0, NZ - 1, NX), (1, 0, 1)):
        edge_rows(flat_v, ZS[0].at[slot, 0], at)
        edge_rows(flat_k, ZS[0].at[slot, 1], at)
        XS0[slot, 0] = V[0, x]
        XS0[slot, 1] = K[x]

    pl.semaphore_wait(barrier, len(greeted))
    everything = []
    sent = copies(0)
    for name in order:
        sent[name].start()
    everything += [sent[name] for name in order]
    for name in order:
        sent[name].wait_recv()
    for slot, x in ((0, 0), (1, NX + 1)):
        V[0, x] = keep(inside[("gx", slot)], XR0[slot, 0])
        K[x] = keep(inside[("gx", slot)], XR0[slot, 1])
        for what in (0, 1):
            ZR[0][slot, what] = keep(inside[("gz", slot)], ZR[0][slot, what])
    edges_k = [keep(inside[("gy", slot)], YR[0][slot, 1]) for slot in (0, 1)]
    edges_v = [keep(inside[("gy", slot)], YR[0][slot, 0]) for slot in (0, 1)]

    put(CX, (0,), tuple((a + b) * 0.5 for a, b in zip(tiles(K, 0), tiles(K, 1))))

    def conds(x, carry):
        here = tiles(K, x + 1)
        for ref, other in (
            (CX.at[x + 1], tiles(K, x + 2)),
            (CZL.at[x], rows_down(here, halo_row(ZR[0], (0, 1), x))),
            (CZH.at[x], rows_up(here, halo_row(ZR[0], (1, 1), x))),
            (CYL.at[x], lanes_down(here, edges_k[0], x)),
            (CYH.at[x], lanes_up(here, edges_k[1], x)),
        ):
            put(ref, (), tuple((a + b) * 0.5 for a, b in zip(here, other)))
        return carry

    loop(conds, 0)

    def stencil(src, zref, zat, edges, write, carry):
        def body(x, state):
            before, inner = state
            here = tiles(src, x + 1)
            after = tuple(c * (n - h) for c, n, h in zip(tiles(CX, x + 1), tiles(src, x + 2), here))
            out = tuple(a - b for a, b in zip(before, after))
            for cond, other in (
                (CZL, rows_down(here, halo_row(zref, zat[0], x))),
                (CZH, rows_up(here, halo_row(zref, zat[1], x))),
                (CYL, lanes_down(here, edges[0], x)),
                (CYH, lanes_up(here, edges[1], x)),
            ):
                out = tuple(o + c * (h - n) for o, c, h, n in zip(out, tiles(cond, x), here, other))
            return after, write(x, out, here, inner)

        first = tuple(c * (n - h) for c, n, h in zip(tiles(CX, 0), tiles(src, 1), tiles(src, 0)))
        return loop(body, (first, carry))[1]

    def advance(phase, edges, zref, zat, with_sums):
        def write(x, out, here, carry):
            put(V, (phase + 1, x + 1), out)
            packed, sums = carry
            packed = pack_edges(out, packed, x)
            if with_sums:
                sums = (
                    sums[0] + here[0] * here[0] + here[1] * here[1],
                    sums[1] + here[0] * out[0] + here[1] * out[1],
                    sums[2] + out[0] * out[0] + out[1] * out[1],
                )
            return packed, sums

        start = ((blank, blank), (blank, blank, blank) if with_sums else ())
        packed, sums = stencil(V.at[phase], zref, zat, edges, write, start)
        YS[1][phase + 1, 0], YS[1][phase + 1, 1] = packed
        return sums

    def send_sum(at, which, values):
        rank, count, peers, ref = (
            (rank_a, count_a, peers_a, RA) if which == 0 else (rank_b, count_b, peers_b, RB)
        )
        RS[at, which] = values
        for peer in peers:
            pltpu.make_async_remote_copy(
                src_ref=RS.at[at, which], dst_ref=ref.at[at, rank], send_sem=red_send.at[at, which],
                recv_sem=red_recv.at[at, which], device_id=peer, device_id_type=MESH,
            ).start()
        ref[at, rank] = values
        whole = ref.at[at, 0:count - 1]
        return pltpu.make_async_remote_copy(
            src_ref=whole, dst_ref=whole, send_sem=red_send.at[at, which], recv_sem=red_recv.at[at, which],
            device_id=peers[0], device_id_type=MESH,
        )

    def end_sum(at, which, waits):
        waits.wait_recv()
        return jnp.sum((RA if which == 0 else RB)[at], axis=0)

    sums = advance(0, edges_v, ZR[0], ((0, 0), (1, 0)), True)
    sent = start_halo(1)
    first_a = send_sum(0, 0, to_row(sums))
    everything += [sent[name] for name in order] + [first_a]

    advance(1, end_halo(1, sent), ZR[1], ((1, 0), (1, 1)), False)
    sent = start_halo(2)
    first_b = send_sum(0, 1, end_sum(0, 0, first_a))
    everything += [sent[name] for name in order] + [first_b]

    advance(2, end_halo(2, sent), ZR[1], ((2, 0), (2, 1)), False)
    sent = start_halo(3)
    everything += [sent[name] for name in order]
    advance(3, end_halo(3, sent), ZR[1], ((3, 0), (3, 1)), False)

    moments = end_sum(0, 1, first_b)
    m0, m1, m2 = (full(moments[:, at:at + 1]) for at in range(3))
    c = m1 / m0
    s2 = jnp.maximum(m2 / m0 - c * c, 0.0)

    def basis(x, carry):
        packed, sums = carry
        powers = [tiles(V, at, x + 1) for at in range(5)]
        fields = []
        for half in (0, 1):
            v = [power[half] for power in powers]
            one = [v[at + 1] - c * v[at] for at in range(4)]
            two = [one[at + 1] - c * one[at] - s2 * v[at] for at in range(3)]
            three = [two[at + 1] - c * two[at] - s2 * one[at] for at in range(2)]
            four = three[1] - c * three[0] - s2 * two[0]
            fields.append((v[0], one[0], two[0], three[0], four))
        for at in range(1, 4):
            put(W, (at - 1, x), (fields[0][at], fields[1][at]))
        last = (fields[0][4], fields[1][4])
        put(V, (4, x + 1), last)
        sums = tuple(
            s + fields[0][i] * fields[0][j] + fields[1][i] * fields[1][j] for s, (i, j) in zip(sums, GRAM)
        )
        return pack_edges(last, packed, x), sums

    packed, sums = loop(basis, ((blank, blank), (blank,) * len(GRAM)))
    second_a = send_sum(1, 0, to_row(sums))
    YS[1][4, 0], YS[1][4, 1] = packed
    sent = start_halo(4)
    everything += [sent[name] for name in order] + [second_a]
    stores = [pltpu.make_async_copy(V.at[0, 1:NX + 1], w_hbm.at[0], out_sem.at[0])]
    stores += [pltpu.make_async_copy(W.at[at - 1], w_hbm.at[at], out_sem.at[at]) for at in range(1, 4)]
    stores += [pltpu.make_async_copy(V.at[4, 1:NX + 1], w_hbm.at[4], out_sem.at[4])]
    for store in stores:
        store.start()

    def last_image(x, out, here, carry):
        put(W, (3, x), out)
        return carry

    stencil(V.at[4], ZR[1], ((4, 0), (4, 1)), end_halo(4, sent), last_image, 0)
    stores += [pltpu.make_async_copy(W.at[3], w_hbm.at[5], out_sem.at[5])]
    stores[-1].start()

    second_b = send_sum(1, 1, end_sum(1, 0, second_a))
    everything += [second_b]
    entries = end_sum(1, 1, second_b)
    gram = {pair: full(entries[:, at:at + 1]) for at, pair in enumerate(GRAM)}
    gram[(0, 0)] = m0
    at = 0
    for part in solve(gram, c, s2):
        for value in part:
            coef_ref[at] = value
            at += 1

    for store in stores:
        store.wait()
    for copy in everything:
        copy.wait_send()


def combine_kernel(w_ref, coef_ref, solution_ref, residual_ref, image_ref, direction_ref):
    for x in range(solution_ref.shape[0]):
        for half in (0, 1):
            at = slice(half * LANES, (half + 1) * LANES)
            w = [w_ref[i, x, half] for i in range(6)]
            start = 0
            for ref, count in ((solution_ref, 4), (residual_ref, 5), (image_ref, 6), (direction_ref, 4)):
                out = coef_ref[start] * w[0]
                for i in range(1, count):
                    out = out + coef_ref[start + i] * w[i]
                ref[x, :, at] = out
                start += count


def shards(right_side, kappa):
    line, plane = 2 * lax.axis_size("gx"), lax.axis_size("gy") * lax.axis_size("gz") // 2
    hbm = pl.BlockSpec(memory_space=pl.ANY)
    vmem = pl.BlockSpec(memory_space=pltpu.VMEM)
    block, inner = (NX, NZ, NY), (NX, 2, NZ, LANES)
    basis, coefs = pl.pallas_call(
        main_kernel,
        out_shape=(jax.ShapeDtypeStruct((6,) + inner, F32), jax.ShapeDtypeStruct((19, NZ, LANES), F32)),
        in_specs=[hbm, hbm],
        out_specs=(hbm, vmem),
        scratch_shapes=[
            pltpu.VMEM((5, NX + 2, 2, NZ, LANES), F32),
            pltpu.VMEM((NX + 2, 2, NZ, LANES), F32),
            pltpu.VMEM((4,) + inner, F32),
            pltpu.VMEM((NX + 1, 2, NZ, LANES), F32),
            pltpu.VMEM(inner, F32),
            pltpu.VMEM(inner, F32),
            pltpu.VMEM(inner, F32),
            pltpu.VMEM(inner, F32),
            pltpu.VMEM((2, 2, 2, NZ, LANES), F32),
            pltpu.VMEM((2, 2, 2, NZ, LANES), F32),
            [pltpu.VMEM((2, 2, 2, NX, LANES), F32), pltpu.VMEM((5, 2, 2, NX, LANES), F32)],
            [pltpu.VMEM((2, 2, 2, NX, LANES), F32), pltpu.VMEM((5, 2, 2, NX, LANES), F32)],
            [pltpu.VMEM((2, 2, NZ, LANES), F32), pltpu.VMEM((5, 2, NZ, LANES), F32)],
            [pltpu.VMEM((2, 2, NZ, LANES), F32), pltpu.VMEM((5, 2, NZ, LANES), F32)],
            pltpu.VMEM((2, 2, 1, LANES), F32),
            pltpu.VMEM((2, line, 1, LANES), F32),
            pltpu.VMEM((2, plane, 1, LANES), F32),
            pltpu.SemaphoreType.DMA((2, 2)),
            pltpu.SemaphoreType.DMA((6,)),
            pltpu.SemaphoreType.DMA((5, 6)),
            pltpu.SemaphoreType.DMA((5, 6)),
            pltpu.SemaphoreType.DMA((2, 2)),
            pltpu.SemaphoreType.DMA((2, 2)),
        ],
        compiler_params=pltpu.CompilerParams(collective_id=0, has_side_effects=True),
        name="basis_and_sums",
    )(right_side, kappa)
    part = 8
    out_block = pl.BlockSpec((part, NZ, NY), lambda i: (i, 0, 0))
    return pl.pallas_call(
        combine_kernel,
        grid=(NX // part,),
        out_shape=(jax.ShapeDtypeStruct(block, F32),) * 4,
        in_specs=[
            pl.BlockSpec((6, part, 2, NZ, LANES), lambda i: (0, i, 0, 0, 0)),
            pl.BlockSpec((19, NZ, LANES), lambda i: (0, 0, 0)),
        ],
        out_specs=(out_block,) * 4,
        name="combine",
    )(basis, coefs)


def solution(mesh):
    placed = P("gx", "gz", "gy")
    return jax.shard_map(
        shards,
        mesh=mesh,
        in_specs=(placed, placed),
        out_specs=(placed,) * 4,
        check_vma=False,
    )
```

```python
import functools

import jax
import jax.numpy as jnp
from jax import lax
from jax.experimental import pallas as pl
from jax.experimental.pallas import tpu as pltpu
from jax.sharding import PartitionSpec as P

MESH = pl.DeviceIdType.MESH
F32 = jnp.float32
NX, NZ, NY = 24, 8, 256
LANES = 128
PART = 12
GRAM = ((0, 1), (0, 2), (0, 3), (1, 1), (1, 2), (1, 3), (2, 2), (2, 3), (3, 3), (3, 4))


def shifted(axis, step):
    count = lax.axis_size(axis)
    return {axis: lax.rem(lax.axis_index(axis) + (step + count), count)}


def ring(step, count):
    return min(step % count, (-step) % count)


def group_line():
    lines = lax.axis_size("gx")
    gx, gz = lax.axis_index("gx"), lax.axis_index("gz")
    core = lax.rem(gz, 2)
    offsets = [(d, c) for d in range(lines) for c in range(2) if (d, c) != (0, 0)]
    offsets.sort(key=lambda o: -(2 * ring(o[0], lines) + o[1]))
    peers = [
        {"gx": lax.rem(gx + d, lines), "gz": gz - core + lax.rem(core + c, 2)} for d, c in offsets
    ]
    return gx * 2 + core, 2 * lines, peers


def group_plane():
    wide, deep = lax.axis_size("gy"), lax.axis_size("gz") // 2
    gy, gz = lax.axis_index("gy"), lax.axis_index("gz")
    offsets = [(d, e) for d in range(deep) for e in range(wide) if (d, e) != (0, 0)]
    offsets.sort(key=lambda o: -(ring(o[0], deep) + ring(o[1], wide)))
    peers = [
        {"gy": lax.rem(gy + e, wide), "gz": lax.rem(gz + 2 * d, 2 * deep)} for d, e in offsets
    ]
    return (gz // 2) * wide + gy, wide * deep, peers


def full(value):
    return jnp.broadcast_to(value, (NZ, LANES))


def total(value):
    return jnp.sum(jnp.sum(value, axis=0, keepdims=True), axis=1, keepdims=True)


def to_row(values):
    lane = lax.broadcasted_iota(jnp.int32, (1, LANES), 1)
    row = jnp.zeros((1, LANES), F32)
    for at, value in enumerate(values):
        row = jnp.where(lane == at, jnp.broadcast_to(total(value), (1, LANES)), row)
    return row


def solve(gram, c, s2):
    zero = jnp.zeros_like(c)
    one = jnp.ones_like(c)

    def g(i, j):
        return gram[(min(i, j), max(i, j))]

    gram = dict(gram)
    gram[(0, 4)] = g(1, 3) - s2 * g(0, 2)
    gram[(1, 4)] = g(2, 3) + s2 * (g(0, 3) - g(1, 2))
    gram[(2, 4)] = g(3, 3) + s2 * (g(1, 3) - g(2, 2))

    def image(a, top):
        out = []
        for i in range(top + 2):
            term = None
            if i <= top:
                term = c * a[i]
            if i >= 1:
                term = a[i - 1] if term is None else term + a[i - 1]
            if i + 1 <= top:
                term = term + s2 * a[i + 1]
            out.append(term)
        return out

    energy = {}
    for i in range(4):
        for j in range(i, 4):
            term = g(i, j + 1) + c * g(i, j)
            if j >= 1:
                term = term + s2 * g(i, j - 1)
            energy[(i, j)] = term

    def form(matrix, a, top):
        out = None
        for i in range(top + 1):
            part = matrix[(i, i)] * a[i]
            for j in range(i + 1, top + 1):
                part = part + (matrix[(i, j)] * 2.0) * a[j]
            out = a[i] * part if out is None else out + a[i] * part
        return out

    rho, way, answer = [one], [], []
    prior_norm = prior_step = None
    for turn in range(4):
        norm_now = form(gram, rho, turn)
        inner = form(energy, rho, turn)
        if turn == 0:
            step = norm_now / inner
            way = list(rho)
        else:
            ratio = norm_now / prior_norm
            step = norm_now / (inner - ratio * norm_now / prior_step)
            way = [rho[i] + ratio * way[i] if i < turn else rho[i] for i in range(turn + 1)]
        answer = [answer[i] + step * way[i] if i < turn else step * way[i] for i in range(turn + 1)]
        moved = image(way, turn)
        rho = [rho[i] - step * moved[i] if i <= turn else zero - step * moved[i] for i in range(turn + 2)]
        prior_norm, prior_step = norm_now, step
    third = image(rho[:4], 3)
    return answer, rho, third + [rho[4]], way


def main_kernel(b_hbm, k_hbm, w_ref, coef_ref,
                V, K, CX, CZL, CZH, CYL, CYH, XS0, XR0, ZS, ZR, YS, YR, RS, RA, RB,
                copy_sem, halo_send, halo_recv, red_send, red_recv):
    gx, gy, gz = lax.axis_index("gx"), lax.axis_index("gy"), lax.axis_index("gz")
    core = lax.rem(gz, 2)
    rank_a, count_a, peers_a = group_line()
    rank_b, count_b, peers_b = group_plane()
    across = {"gz": lax.rem(gz + 2 * core - 1 + lax.axis_size("gz"), lax.axis_size("gz"))}

    loads = []
    for half in (0, 1):
        at = slice(half * LANES, (half + 1) * LANES)
        loads.append(pltpu.make_async_copy(b_hbm.at[:, :, at], V.at[0, 1:NX + 1, half], copy_sem.at[0, half]))
        loads.append(pltpu.make_async_copy(k_hbm.at[:, :, at], K.at[1:NX + 1, half], copy_sem.at[1, half]))
    for load in loads:
        load.start()

    barrier = pltpu.get_barrier_semaphore()
    greeted = peers_b + peers_a + [across]
    for peer in greeted:
        pl.semaphore_signal(barrier, inc=1, device_id=peer, device_id_type=MESH)

    lane = lax.broadcasted_iota(jnp.int32, (NZ, LANES), 1)
    row = lax.broadcasted_iota(jnp.int32, (NZ, LANES), 0)
    inside = {
        ("gx", 0): gx > 0, ("gx", 1): gx < lax.axis_size("gx") - 1,
        ("gy", 0): gy > 0, ("gy", 1): gy < lax.axis_size("gy") - 1,
        ("gz", 0): gz > 0, ("gz", 1): gz < lax.axis_size("gz") - 1,
    }
    target = {
        (axis, slot): shifted(axis, 1 if slot == 0 else -1) for axis in ("gx", "gy", "gz") for slot in (0, 1)
    }
    order = [("gz", 0), ("gz", 1), ("gx", 0), ("gx", 1), ("gy", 0), ("gy", 1)]

    def copies(phase):
        out = {}
        for at, (axis, slot) in enumerate(order):
            if axis == "gx":
                if phase == 0:
                    src, dst = XS0.at[slot], XR0.at[slot]
                else:
                    src = V.at[phase, NX if slot == 0 else 1]
                    dst = V.at[phase, 0 if slot == 0 else NX + 1]
            elif axis == "gz":
                src, dst = ZS[min(phase, 1)], ZR[min(phase, 1)]
                src, dst = (src.at[slot], dst.at[slot]) if phase == 0 else (src.at[phase, slot], dst.at[phase, slot])
            else:
                src, dst = YS[min(phase, 1)], YR[min(phase, 1)]
                src, dst = (src.at[slot], dst.at[slot]) if phase == 0 else (src.at[phase, slot], dst.at[phase, slot])
            out[(axis, slot)] = pltpu.make_async_remote_copy(
                src_ref=src, dst_ref=dst, send_sem=halo_send.at[phase, at], recv_sem=halo_recv.at[phase, at],
                device_id=target[(axis, slot)], device_id_type=MESH,
            )
        return out

    def edge_rows(flat, dst, at):
        for half in (0, 1):
            dst[half] = flat[pl.ds(2 * NZ + half * NZ + at, NX, stride=2 * NZ), :]

    def start_halo(phase):
        flat = V.at[phase].reshape((NX + 2) * 2 * NZ, LANES)
        edge_rows(flat, ZS[1].at[phase, 0], NZ - 1)
        edge_rows(flat, ZS[1].at[phase, 1], 0)
        sent = copies(phase)
        for name in order:
            sent[name].start()
        return sent

    def keep(flag, value):
        return jnp.where(flag, value, jnp.zeros_like(value))

    def end_halo(phase, sent):
        for name in order:
            sent[name].wait_recv()
        V[phase, 0] = keep(inside[("gx", 0)], V[phase, 0])
        V[phase, NX + 1] = keep(inside[("gx", 1)], V[phase, NX + 1])
        for slot in (0, 1):
            ZR[1][phase, slot] = keep(inside[("gz", slot)], ZR[1][phase, slot])
        return [keep(inside[("gy", slot)], YR[1][phase, slot]) for slot in (0, 1)]

    def tiles(ref, *at):
        return ref[(*at, 0)], ref[(*at, 1)]

    def put(ref, at, pair):
        ref[(*at, 0)], ref[(*at, 1)] = pair

    def lanes_down(pair, packed, x):
        first, second = pltpu.roll(pair[0], 1, 1), pltpu.roll(pair[1], 1, 1)
        edge = pltpu.roll(packed, lax.rem(LANES - x, LANES), 1)
        return jnp.where(lane == 0, edge, first), jnp.where(lane == 0, first, second)

    def lanes_up(pair, packed, x):
        first, second = pltpu.roll(pair[0], LANES - 1, 1), pltpu.roll(pair[1], LANES - 1, 1)
        edge = pltpu.roll(packed, LANES - 1 - x, 1)
        return jnp.where(lane == LANES - 1, second, first), jnp.where(lane == LANES - 1, edge, second)

    def rows_down(pair, halo):
        return tuple(jnp.where(row == 0, full(h), pltpu.roll(p, 1, 0)) for p, h in zip(pair, halo))

    def rows_up(pair, halo):
        return tuple(jnp.where(row == NZ - 1, full(h), pltpu.roll(p, NZ - 1, 0)) for p, h in zip(pair, halo))

    def halo_row(ref, at, x):
        return tuple(ref[(*at, half, pl.ds(x, 1), slice(None))] for half in (0, 1))

    def pack_edges(pair, packed, x):
        up = jnp.where(lane == x, pltpu.roll(pair[1], lax.rem(x + 1, LANES), 1), packed[0])
        down = jnp.where(lane == x, pltpu.roll(pair[0], x, 1), packed[1])
        return up, down

    blank = jnp.zeros((NZ, LANES), F32)

    def loop(body, carry):
        return lax.fori_loop(0, NX, body, carry, unroll=True)

    for load in loads:
        load.wait()

    def pack_both(x, packed):
        field = pack_edges(tiles(V, 0, x + 1), packed[:2], x)
        coeff = pack_edges(tiles(K, x + 1), packed[2:], x)
        return field + coeff

    packed = loop(pack_both, (blank,) * 4)
    YS[0][0, 0], YS[0][1, 0], YS[0][0, 1], YS[0][1, 1] = packed
    flat_v = V.at[0].reshape((NX + 2) * 2 * NZ, LANES)
    flat_k = K.reshape((NX + 2) * 2 * NZ, LANES)
    for slot, at, x in ((0, NZ - 1, NX), (1, 0, 1)):
        edge_rows(flat_v, ZS[0].at[slot, 0], at)
        edge_rows(flat_k, ZS[0].at[slot, 1], at)
        XS0[slot, 0] = V[0, x]
        XS0[slot, 1] = K[x]

    pl.semaphore_wait(barrier, len(greeted))
    everything = []
    sent = copies(0)
    for name in order:
        sent[name].start()
    everything += [sent[name] for name in order]
    for name in order:
        sent[name].wait_recv()
    for slot, x in ((0, 0), (1, NX + 1)):
        V[0, x] = keep(inside[("gx", slot)], XR0[slot, 0])
        K[x] = keep(inside[("gx", slot)], XR0[slot, 1])
        for what in (0, 1):
            ZR[0][slot, what] = keep(inside[("gz", slot)], ZR[0][slot, what])
    edges_k = [keep(inside[("gy", slot)], YR[0][slot, 1]) for slot in (0, 1)]
    edges_v = [keep(inside[("gy", slot)], YR[0][slot, 0]) for slot in (0, 1)]

    put(CX, (0,), tuple((a + b) * 0.5 for a, b in zip(tiles(K, 0), tiles(K, 1))))

    def conds(x, carry):
        here = tiles(K, x + 1)
        for ref, other in (
            (CX.at[x + 1], tiles(K, x + 2)),
            (CZL.at[x], rows_down(here, halo_row(ZR[0], (0, 1), x))),
            (CZH.at[x], rows_up(here, halo_row(ZR[0], (1, 1), x))),
            (CYL.at[x], lanes_down(here, edges_k[0], x)),
            (CYH.at[x], lanes_up(here, edges_k[1], x)),
        ):
            put(ref, (), tuple((a + b) * 0.5 for a, b in zip(here, other)))
        return carry

    loop(conds, 0)

    def stencil(src, zref, zat, edges, write, carry):
        def body(x, state):
            before, inner = state
            here = tiles(src, x + 1)
            after = tuple(c * (n - h) for c, n, h in zip(tiles(CX, x + 1), tiles(src, x + 2), here))
            out = tuple(a - b for a, b in zip(before, after))
            for cond, other in (
                (CZL, rows_down(here, halo_row(zref, zat[0], x))),
                (CZH, rows_up(here, halo_row(zref, zat[1], x))),
                (CYL, lanes_down(here, edges[0], x)),
                (CYH, lanes_up(here, edges[1], x)),
            ):
                out = tuple(o + c * (h - n) for o, c, h, n in zip(out, tiles(cond, x), here, other))
            return after, write(x, out, here, inner)

        first = tuple(c * (n - h) for c, n, h in zip(tiles(CX, 0), tiles(src, 1), tiles(src, 0)))
        return loop(body, (first, carry))[1]

    def advance(phase, edges, zref, zat, with_sums):
        def write(x, out, here, carry):
            put(V, (phase + 1, x + 1), out)
            packed, sums = carry
            packed = pack_edges(out, packed, x)
            if with_sums:
                sums = (
                    sums[0] + here[0] * here[0] + here[1] * here[1],
                    sums[1] + here[0] * out[0] + here[1] * out[1],
                    sums[2] + out[0] * out[0] + out[1] * out[1],
                )
            return packed, sums

        start = ((blank, blank), (blank, blank, blank) if with_sums else ())
        packed, sums = stencil(V.at[phase], zref, zat, edges, write, start)
        YS[1][phase + 1, 0], YS[1][phase + 1, 1] = packed
        return sums

    def send_sum(at, which, values):
        rank, count, peers, ref = (
            (rank_a, count_a, peers_a, RA) if which == 0 else (rank_b, count_b, peers_b, RB)
        )
        RS[at, which] = values
        for peer in peers:
            pltpu.make_async_remote_copy(
                src_ref=RS.at[at, which], dst_ref=ref.at[at, rank], send_sem=red_send.at[at, which],
                recv_sem=red_recv.at[at, which], device_id=peer, device_id_type=MESH,
            ).start()
        ref[at, rank] = values
        whole = ref.at[at, 0:count - 1]
        return pltpu.make_async_remote_copy(
            src_ref=whole, dst_ref=whole, send_sem=red_send.at[at, which], recv_sem=red_recv.at[at, which],
            device_id=peers[0], device_id_type=MESH,
        )

    def end_sum(at, which, waits):
        waits.wait_recv()
        return jnp.sum((RA if which == 0 else RB)[at], axis=0)

    sums = advance(0, edges_v, ZR[0], ((0, 0), (1, 0)), True)
    sent = start_halo(1)
    first_a = send_sum(0, 0, to_row(sums))
    everything += [sent[name] for name in order] + [first_a]

    advance(1, end_halo(1, sent), ZR[1], ((1, 0), (1, 1)), False)
    sent = start_halo(2)
    first_b = send_sum(0, 1, end_sum(0, 0, first_a))
    everything += [sent[name] for name in order] + [first_b]

    advance(2, end_halo(2, sent), ZR[1], ((2, 0), (2, 1)), False)
    sent = start_halo(3)
    everything += [sent[name] for name in order]
    advance(3, end_halo(3, sent), ZR[1], ((3, 0), (3, 1)), False)

    moments = end_sum(0, 1, first_b)
    m0, m1, m2 = (full(moments[:, at:at + 1]) for at in range(3))
    c = m1 / m0
    s2 = jnp.maximum(m2 / m0 - c * c, 0.0)

    def basis(x, carry):
        packed, sums = carry
        powers = [tiles(V, at, x + 1) for at in range(5)]
        fields = []
        for half in (0, 1):
            v = [power[half] for power in powers]
            one = [v[at + 1] - c * v[at] for at in range(4)]
            two = [one[at + 1] - c * one[at] - s2 * v[at] for at in range(3)]
            three = [two[at + 1] - c * two[at] - s2 * one[at] for at in range(2)]
            four = three[1] - c * three[0] - s2 * two[0]
            fields.append((v[0], one[0], two[0], three[0], four))
        for at in range(1, 4):
            put(w_ref, (at, x), (fields[0][at], fields[1][at]))
        last = (fields[0][4], fields[1][4])
        put(V, (4, x + 1), last)
        put(w_ref, (0, x), (fields[0][0], fields[1][0]))
        put(w_ref, (4, x), last)
        sums = tuple(
            s + fields[0][i] * fields[0][j] + fields[1][i] * fields[1][j] for s, (i, j) in zip(sums, GRAM)
        )
        return pack_edges(last, packed, x), sums

    packed, sums = loop(basis, ((blank, blank), (blank,) * len(GRAM)))
    second_a = send_sum(1, 0, to_row(sums))
    YS[1][4, 0], YS[1][4, 1] = packed
    sent = start_halo(4)
    everything += [sent[name] for name in order] + [second_a]

    def last_image(x, out, here, carry):
        put(w_ref, (5, x), out)
        return carry

    stencil(V.at[4], ZR[1], ((4, 0), (4, 1)), end_halo(4, sent), last_image, 0)
    second_b = send_sum(1, 1, end_sum(1, 0, second_a))
    everything += [second_b]
    entries = end_sum(1, 1, second_b)
    gram = {pair: full(entries[:, at:at + 1]) for at, pair in enumerate(GRAM)}
    gram[(0, 0)] = m0
    at = 0
    for part in solve(gram, c, s2):
        for value in part:
            coef_ref[at] = value
            at += 1

    for copy in everything:
        copy.wait_send()


def combine_kernel(w_ref, coef_ref, solution_ref, residual_ref, image_ref, direction_ref, held, sems):
    refs = (solution_ref, residual_ref, image_ref, direction_ref)
    copies = []
    for part in range(NX // PART):
        for x in range(part * PART, (part + 1) * PART):
            for half in (0, 1):
                at = slice(half * LANES, (half + 1) * LANES)
                w = [w_ref[i, x, half] for i in range(6)]
                start = 0
                for which, count in enumerate((4, 5, 6, 4)):
                    out = coef_ref[start] * w[0]
                    for i in range(1, count):
                        out = out + coef_ref[start + i] * w[i]
                    held[which, x, :, at] = out
                    start += count
        rows = pl.ds(part * PART, PART)
        for which, ref in enumerate(refs):
            copies.append(pltpu.make_async_copy(held.at[which, rows], ref.at[rows], sems.at[which, part]))
            copies[-1].start()
    for copy in copies:
        copy.wait()


def shards(right_side, kappa):
    line, plane = 2 * lax.axis_size("gx"), lax.axis_size("gy") * lax.axis_size("gz") // 2
    hbm = pl.BlockSpec(memory_space=pltpu.MemorySpace.HBM)
    vmem = pl.BlockSpec(memory_space=pltpu.VMEM)
    block, inner = (NX, NZ, NY), (NX, 2, NZ, LANES)
    basis, coefs = pl.pallas_call(
        main_kernel,
        out_shape=(pltpu.VMEM((6,) + inner, F32), pltpu.VMEM((19, NZ, LANES), F32)),
        in_specs=[hbm, hbm],
        out_specs=(vmem, vmem),
        scratch_shapes=[
            pltpu.VMEM((5, NX + 2, 2, NZ, LANES), F32),
            pltpu.VMEM((NX + 2, 2, NZ, LANES), F32),
            pltpu.VMEM((NX + 1, 2, NZ, LANES), F32),
            pltpu.VMEM(inner, F32),
            pltpu.VMEM(inner, F32),
            pltpu.VMEM(inner, F32),
            pltpu.VMEM(inner, F32),
            pltpu.VMEM((2, 2, 2, NZ, LANES), F32),
            pltpu.VMEM((2, 2, 2, NZ, LANES), F32),
            [pltpu.VMEM((2, 2, 2, NX, LANES), F32), pltpu.VMEM((5, 2, 2, NX, LANES), F32)],
            [pltpu.VMEM((2, 2, 2, NX, LANES), F32), pltpu.VMEM((5, 2, 2, NX, LANES), F32)],
            [pltpu.VMEM((2, 2, NZ, LANES), F32), pltpu.VMEM((5, 2, NZ, LANES), F32)],
            [pltpu.VMEM((2, 2, NZ, LANES), F32), pltpu.VMEM((5, 2, NZ, LANES), F32)],
            pltpu.VMEM((2, 2, 1, LANES), F32),
            pltpu.VMEM((2, line, 1, LANES), F32),
            pltpu.VMEM((2, plane, 1, LANES), F32),
            pltpu.SemaphoreType.DMA((2, 2)),
            pltpu.SemaphoreType.DMA((5, 6)),
            pltpu.SemaphoreType.DMA((5, 6)),
            pltpu.SemaphoreType.DMA((2, 2)),
            pltpu.SemaphoreType.DMA((2, 2)),
        ],
        compiler_params=pltpu.CompilerParams(collective_id=0, has_side_effects=True, vmem_limit_bytes=60 * 2**20),
        name="basis_and_sums",
    )(right_side, kappa)
    return pl.pallas_call(
        combine_kernel,
        out_shape=(jax.ShapeDtypeStruct(block, F32),) * 4,
        in_specs=[vmem, vmem],
        out_specs=(hbm,) * 4,
        scratch_shapes=[pltpu.VMEM((4,) + block, F32), pltpu.SemaphoreType.DMA((4, NX // PART))],
        compiler_params=pltpu.CompilerParams(vmem_limit_bytes=8 * 2**20),
        name="combine",
    )(basis, coefs)


def solution(mesh):
    placed = P("gx", "gz", "gy")
    return jax.shard_map(
        shards,
        mesh=mesh,
        in_specs=(placed, placed),
        out_specs=(placed,) * 4,
        check_vma=False,
    )
```

```python
import functools

import jax
import jax.numpy as jnp
from jax import lax
from jax.experimental import pallas as pl
from jax.experimental.pallas import tpu as pltpu
from jax.sharding import PartitionSpec as P

MESH = pl.DeviceIdType.MESH
F32 = jnp.float32
NX, NZ, NY = 24, 8, 256
LANES = 128
PART = 12
GROUP = 32
GRAM = ((0, 0), (0, 1), (0, 2), (0, 3), (1, 1), (1, 2), (1, 3), (2, 2), (2, 3), (3, 3), (3, 4))


def shifted(axis, step):
    count = lax.axis_size(axis)
    return {axis: lax.rem(lax.axis_index(axis) + (step + count), count)}


def ring(step, count):
    return min(step % count, (-step) % count)


def group_line():
    lines = lax.axis_size("gx")
    gx, gz = lax.axis_index("gx"), lax.axis_index("gz")
    core = lax.rem(gz, 2)
    offsets = [(d, c) for d in range(lines) for c in range(2) if (d, c) != (0, 0)]
    offsets.sort(key=lambda o: -(2 * ring(o[0], lines) + o[1]))
    peers = [
        {"gx": lax.rem(gx + d, lines), "gz": gz - core + lax.rem(core + c, 2)} for d, c in offsets
    ]
    return gx * 2 + core, 2 * lines, peers


def group_plane():
    wide, deep = lax.axis_size("gy"), lax.axis_size("gz") // 2
    gy, gz = lax.axis_index("gy"), lax.axis_index("gz")
    offsets = [(d, e) for d in range(deep) for e in range(wide) if (d, e) != (0, 0)]
    offsets.sort(key=lambda o: -(ring(o[0], deep) + ring(o[1], wide)))
    peers = [
        {"gy": lax.rem(gy + e, wide), "gz": lax.rem(gz + 2 * d, 2 * deep)} for d, e in offsets
    ]
    return (gz // 2) * wide + gy, wide * deep, peers


def full(value):
    return jnp.broadcast_to(value, (NZ, LANES))


def total(value):
    return jnp.sum(jnp.sum(value, axis=0, keepdims=True), axis=1, keepdims=True)


def to_row(values):
    lane = lax.broadcasted_iota(jnp.int32, (1, LANES), 1)
    row = jnp.zeros((1, LANES), F32)
    for at, value in enumerate(values):
        row = jnp.where(lane == at, jnp.broadcast_to(total(value), (1, LANES)), row)
    return row


def solve(gram, c, s2):
    zero = jnp.zeros_like(c)
    one = jnp.ones_like(c)

    def g(i, j):
        return gram[(min(i, j), max(i, j))]

    gram = dict(gram)
    gram[(0, 4)] = g(1, 3) - s2 * g(0, 2)
    gram[(1, 4)] = g(2, 3) + s2 * (g(0, 3) - g(1, 2))
    gram[(2, 4)] = g(3, 3) + s2 * (g(1, 3) - g(2, 2))

    def image(a, top):
        out = []
        for i in range(top + 2):
            term = None
            if i <= top:
                term = c * a[i]
            if i >= 1:
                term = a[i - 1] if term is None else term + a[i - 1]
            if i + 1 <= top:
                term = term + s2 * a[i + 1]
            out.append(term)
        return out

    energy = {}
    for i in range(4):
        for j in range(i, 4):
            term = g(i, j + 1) + c * g(i, j)
            if j >= 1:
                term = term + s2 * g(i, j - 1)
            energy[(i, j)] = term

    def form(matrix, a, top):
        out = None
        for i in range(top + 1):
            part = matrix[(i, i)] * a[i]
            for j in range(i + 1, top + 1):
                part = part + (matrix[(i, j)] * 2.0) * a[j]
            out = a[i] * part if out is None else out + a[i] * part
        return out

    rho, way, answer = [one], [], []
    prior_norm = prior_step = None
    for turn in range(4):
        norm_now = form(gram, rho, turn)
        inner = form(energy, rho, turn)
        if turn == 0:
            step = norm_now / inner
            way = list(rho)
        else:
            ratio = norm_now / prior_norm
            step = norm_now / (inner - ratio * norm_now / prior_step)
            way = [rho[i] + ratio * way[i] if i < turn else rho[i] for i in range(turn + 1)]
        answer = [answer[i] + step * way[i] if i < turn else step * way[i] for i in range(turn + 1)]
        moved = image(way, turn)
        rho = [rho[i] - step * moved[i] if i <= turn else zero - step * moved[i] for i in range(turn + 2)]
        prior_norm, prior_step = norm_now, step
    third = image(rho[:4], 3)
    return answer, rho, third + [rho[4]], way


def main_kernel(b_hbm, k_hbm, w_ref, coef_ref,
                V, CX, CZL, CZH, CYL, CYH, GX, GZ, GY, ZS, ZR, YS, YR, XZ, ZY, XY, RS, RA, RB,
                copy_sem, halo_send, halo_recv, red_send, red_recv):
    gx, gy, gz = lax.axis_index("gx"), lax.axis_index("gy"), lax.axis_index("gz")
    core = lax.rem(gz, 2)
    rank_a, count_a, peers_a = group_line()
    rank_b, count_b, peers_b = group_plane()
    across = {"gz": lax.rem(gz + 2 * core - 1 + lax.axis_size("gz"), lax.axis_size("gz"))}
    pairs = (("gx", "gz"), ("gz", "gy"), ("gx", "gy"))
    slots = (0, 1)
    target, inside = {}, {}
    for axis, at in (("gx", gx), ("gy", gy), ("gz", gz)):
        for slot in slots:
            target[(axis, slot)] = shifted(axis, 1 - 2 * slot)
        inside[(axis, 0)], inside[(axis, 1)] = at > 0, at < lax.axis_size(axis) - 1
    corners = [(p, i, q, j) for p, q in pairs for i in slots for j in slots]
    for p, i, q, j in corners:
        target[(p, i, q, j)] = {**target[(p, i)], **target[(q, j)]}
        inside[(p, i, q, j)] = jnp.logical_and(inside[(p, i)], inside[(q, j)])

    loads = []
    for half in (0, 1):
        at = slice(half * LANES, (half + 1) * LANES)
        for what, ref in ((1, b_hbm), (0, k_hbm)):
            loads.append(pltpu.make_async_copy(ref.at[:, :, at], V.at[what, 2:NX + 2, half], copy_sem.at[what, half]))
    for load in loads:
        load.start()

    barrier = pltpu.get_barrier_semaphore()
    greeted = peers_b + peers_a + [target[corner] for corner in corners] + [across]
    for peer in greeted:
        pl.semaphore_signal(barrier, inc=1, device_id=peer, device_id_type=MESH)

    lane = lax.broadcasted_iota(jnp.int32, (NZ, LANES), 1)
    row = lax.broadcasted_iota(jnp.int32, (NZ, LANES), 0)
    lane_x = lax.broadcasted_iota(jnp.int32, (NX, LANES), 1)
    row_x = lax.broadcasted_iota(jnp.int32, (NX, LANES), 0)
    blank = jnp.zeros((NZ, LANES), F32)
    everything = []

    def faces():
        return [("gz", 0), ("gz", 1)], [("gx", 0), ("gx", 1), ("gy", 0), ("gy", 1)]

    def start_halo(phase, first, count, depth):
        what = pl.ds(first, count)
        ends = {}
        for slot in slots:
            low = NX + 2 - depth if slot == 0 else 2
            ghost = 2 - depth if slot == 0 else NX + 2
            ends[("gx", slot)] = V.at[what, low:low + depth], V.at[what, ghost:ghost + depth]
            ends[("gz", slot)] = ZS.at[what, slot, 0:depth], ZR.at[what, slot, 0:depth]
            ends[("gy", slot)] = YS.at[phase, slot], YR.at[phase, slot]
        for i in slots if depth == 2 else ():
            for j in slots:
                at = NX - 1 if i == 0 else 0
                ends[("gx", i, "gz", j)] = ZS.at[what, j, 0, :, at:at + 1], XZ.at[what, i, j, :, at:at + 1]
                at = NZ - 1 if i == 0 else 0
                ends[("gz", i, "gy", j)] = YS.at[phase, j, at:at + 1], ZY.at[phase, i, j, at:at + 1]
                ends[("gx", i, "gy", j)] = YS.at[phase, j], XY.at[phase, i, j]
        head, tail = faces()
        order = head + (corners if depth == 2 else []) + tail
        sent = []
        for at, name in enumerate(order):
            src, dst = ends[name]
            sent.append(pltpu.make_async_remote_copy(
                src_ref=src, dst_ref=dst, send_sem=halo_send.at[phase, at], recv_sem=halo_recv.at[phase, at],
                device_id=target[name], device_id_type=MESH,
            ))
            sent[-1].start()
        everything.extend(sent)
        return sent

    def keep(flag, value):
        return jnp.where(flag, value, jnp.zeros_like(value))

    def end_halo(sent, first, count, depth):
        for copy in sent:
            copy.wait_recv()
        for what in range(first, first + count):
            for slot in slots:
                for layer in range(depth):
                    at = 1 - layer if slot == 0 else NX + 2 + layer
                    V[what, at] = keep(inside[("gx", slot)], V[what, at])
                    ZR[what, slot, layer] = keep(inside[("gz", slot)], ZR[what, slot, layer])

    def tiles(ref, *at):
        return ref[(*at, 0)], ref[(*at, 1)]

    def put(ref, at, pair):
        ref[(*at, 0)], ref[(*at, 1)] = pair

    def turned(value, by):
        return pltpu.roll(value, by % LANES, 1)

    def lanes_down(pair, packed, x):
        first, second = turned(pair[0], 1), turned(pair[1], 1)
        edge = pltpu.roll(packed, lax.rem(LANES - x, LANES), 1)
        return jnp.where(lane == 0, edge, first), jnp.where(lane == 0, first, second)

    def lanes_up(pair, packed, x):
        first, second = turned(pair[0], -1), turned(pair[1], -1)
        edge = pltpu.roll(packed, LANES - 1 - x, 1)
        return jnp.where(lane == LANES - 1, second, first), jnp.where(lane == LANES - 1, edge, second)

    def rows_down(pair, halo):
        return tuple(jnp.where(row == 0, full(h), pltpu.roll(p, 1, 0)) for p, h in zip(pair, halo))

    def rows_up(pair, halo):
        return tuple(jnp.where(row == NZ - 1, full(h), pltpu.roll(p, NZ - 1, 0)) for p, h in zip(pair, halo))

    def halo_row(what, slot, x):
        return tuple(ZR[what, slot, 0, half, pl.ds(x, 1), :] for half in (0, 1))

    def loop(body, carry):
        return lax.fori_loop(0, NX, body, carry, unroll=True)

    def pack_rows(what, depth):
        flat = V.at[what].reshape((NX + 4) * 2 * NZ, LANES)
        for slot in slots:
            for layer in range(depth):
                at = NZ - 1 - layer if slot == 0 else layer
                for half in (0, 1):
                    ZS[what, slot, layer, half] = flat[pl.ds((4 + half) * NZ + at, NX, stride=2 * NZ), :]

    def pack_lanes(pair, packed, x, start, depth):
        up, down = packed
        for layer in range(depth):
            at = start + GROUP * layer
            here = lane == x + at
            up = jnp.where(here, pltpu.roll(pair[1], lax.rem(x + at + 1 + layer, LANES), 1), up)
            down = jnp.where(here, pltpu.roll(pair[0], lax.rem(x + at + LANES - layer, LANES), 1), down)
        return up, down

    def y_tile(phase, slot, start):
        return turned(keep(inside[("gy", slot)], YR[phase, slot]), -start)

    def ghosts_x(phase, what, start, slot):
        at = 1 if slot == 0 else NX + 2
        x = NX - 1 if slot == 0 else 0
        here = tiles(V, what, at)
        lines = [
            tuple(keep(inside[("gx", slot, "gz", j)], XZ[what, slot, j, half, x:x + 1, :]) for half in (0, 1))
            for j in slots
        ]
        sides = [turned(keep(inside[("gx", slot, "gy", j)], XY[phase, slot, j]), -start) for j in slots]
        return here, (
            tiles(V, what, at - 1), tiles(V, what, at + 1), rows_down(here, lines[0]), rows_up(here, lines[1]),
            lanes_down(here, sides[0], x), lanes_up(here, sides[1], x),
        )

    def ghosts_z(phase, what, start, slot):
        here, outer, inner = tiles(ZR, what, slot, 0), tiles(ZR, what, slot, 1), tiles(ZS, what, 1 - slot, 0)

        def line(i, half):
            at = NX - 1 if i == 0 else 0
            value = keep(inside[("gx", i, "gz", slot)], XZ[what, i, slot, half, at:at + 1, :])
            return jnp.broadcast_to(value, (NX, LANES))

        def column(j):
            at = NZ - 1 if slot == 0 else 0
            value = keep(inside[("gz", slot, "gy", j)], ZY[phase, slot, j, at:at + 1, :])
            spread = jnp.where(lane_x == row_x + start, jnp.broadcast_to(value, (NX, LANES)), 0.0)
            return jnp.broadcast_to(jnp.sum(spread, axis=1, keepdims=True), (NX, LANES))

        before = tuple(jnp.where(row_x == 0, line(0, half), pltpu.roll(here[half], 1, 0)) for half in (0, 1))
        after = tuple(jnp.where(row_x == NX - 1, line(1, half), pltpu.roll(here[half], NX - 1, 0)) for half in (0, 1))
        down = [turned(here[half], 1) for half in (0, 1)]
        up = [turned(here[half], -1) for half in (0, 1)]
        left = jnp.where(lane_x == 0, column(0), down[0]), jnp.where(lane_x == 0, down[0], down[1])
        last = lane_x == LANES - 1
        right = jnp.where(last, up[1], up[0]), jnp.where(last, column(1), up[1])
        return here, (before, after, outer, inner, left, right)

    def ghosts_y(phase, what, start, slot):
        here = y_tile(phase, slot, start)
        outer = y_tile(phase, slot, start + GROUP)
        inner = turned(YS[phase, 1 - slot], -start)
        lines, sides = [], []
        for i in slots:
            at = NZ - 1 if i == 0 else 0
            value = keep(inside[("gz", i, "gy", slot)], ZY[phase, i, slot, at:at + 1, :])
            lines.append(turned(full(value), -start))
            value = turned(keep(inside[("gx", i, "gy", slot)], XY[phase, i, slot]), -start)
            sides.append(turned(value, 1 - NX if i == 0 else NX - 1))
        before = jnp.where(lane == 0, sides[0], turned(here, 1))
        after = jnp.where(lane == NX - 1, sides[1], turned(here, -1))
        low = jnp.where(row == 0, lines[0], pltpu.roll(here, 1, 0))
        high = jnp.where(row == NZ - 1, lines[1], pltpu.roll(here, NZ - 1, 0))
        return (here,), ((before,), (after,), (low,), (high,), (outer,), (inner,))

    regions = ((ghosts_x, GX, "gx"), (ghosts_z, GZ, "gz"), (ghosts_y, GY, "gy"))

    def ghost_conds():
        for find, ref, _ in regions:
            for slot in slots:
                here, others = find(0, 0, 0, slot)
                for at, other in enumerate(others):
                    for part, (a, b) in enumerate(zip(here, other)):
                        ref[slot, at, part] = (a + b) * 0.5

    def ghost_image(phase, what, start):
        sides = []
        for find, ref, axis in regions:
            for slot in slots:
                here, others = find(phase, what, start, slot)
                out = [None] * len(here)
                for at, other in enumerate(others):
                    for part, (a, b) in enumerate(zip(here, other)):
                        term = ref[slot, at, part] * (a - b)
                        out[part] = term if out[part] is None else out[part] + term
                out = tuple(keep(inside[(axis, slot)], value) for value in out)
                if axis == "gx":
                    put(V, (what + 1, 1 if slot == 0 else NX + 2), out)
                elif axis == "gz":
                    put(ZR, (what + 1, slot, 0), out)
                else:
                    sides.append(out[0])
        return sides

    for load in loads:
        load.wait()

    def pack_both(x, packed):
        for what in (0, 1):
            packed = pack_lanes(tiles(V, what, x + 2), packed, x, 2 * GROUP * what, 2)
        return packed

    packed = loop(pack_both, (blank, blank))
    YS[0, 0], YS[0, 1] = packed
    for what in (0, 1):
        pack_rows(what, 2)
    pl.semaphore_wait(barrier, len(greeted))
    sent = start_halo(0, 0, 2, 2)

    def own_part(x, state):
        before, sums = state
        here, coeff = tiles(V, 1, x + 2), tiles(V, 0, x + 2)
        after = tuple(
            (a + b) * 0.5 * (n - h)
            for a, b, n, h in zip(coeff, tiles(V, 0, x + 3), tiles(V, 1, x + 3), here)
        )
        after = tuple(jnp.where(x < NX - 1, value, 0.0) for value in after)
        out = tuple(a - b for a, b in zip(before, after))
        for shift, edge in ((1, 0), (NZ - 1, NZ - 1)):
            out = tuple(
                o + jnp.where(row == edge, 0.0, (k + pltpu.roll(k, shift, 0)) * 0.5 * (h - pltpu.roll(h, shift, 0)))
                for o, k, h in zip(out, coeff, here)
            )
        for shift, edge, end in ((1, 0, 0), (-1, LANES - 1, 1)):
            k_turn, h_turn = [turned(k, shift) for k in coeff], [turned(h, shift) for h in here]
            terms = []
            for half in (0, 1):
                k_next = k_turn[half] if half == end else jnp.where(lane == edge, k_turn[1 - half], k_turn[half])
                h_next = h_turn[half] if half == end else jnp.where(lane == edge, h_turn[1 - half], h_turn[half])
                term = (coeff[half] + k_next) * 0.5 * (here[half] - h_next)
                terms.append(jnp.where(lane == edge, 0.0, term) if half == end else term)
            out = tuple(o + t for o, t in zip(out, terms))
        sums = (
            sums[0] + here[0] * here[0] + here[1] * here[1],
            sums[1] + here[0] * out[0] + here[1] * out[1],
            sums[2] + out[0] * out[0] + out[1] * out[1],
        )
        return after, sums

    def send_sum(at, which, values):
        rank, count, peers, ref = (
            (rank_a, count_a, peers_a, RA) if which == 0 else (rank_b, count_b, peers_b, RB)
        )
        RS[at, which] = values
        for peer in peers:
            pltpu.make_async_remote_copy(
                src_ref=RS.at[at, which], dst_ref=ref.at[at, rank], send_sem=red_send.at[at, which],
                recv_sem=red_recv.at[at, which], device_id=peer, device_id_type=MESH,
            ).start()
        ref[at, rank] = values
        whole = ref.at[at, 0:count - 1]
        waits = pltpu.make_async_remote_copy(
            src_ref=whole, dst_ref=whole, send_sem=red_send.at[at, which], recv_sem=red_recv.at[at, which],
            device_id=peers[0], device_id_type=MESH,
        )
        everything.append(waits)
        return waits

    def end_sum(at, which, waits):
        waits.wait_recv()
        return jnp.sum((RA if which == 0 else RB)[at], axis=0)

    sums = loop(own_part, ((blank, blank), (blank, blank, blank)))[1]
    first_a = send_sum(0, 0, to_row(sums))
    end_halo(sent, 0, 2, 2)

    put(CX, (0,), tuple((a + b) * 0.5 for a, b in zip(tiles(V, 0, 1), tiles(V, 0, 2))))
    edges_k = [y_tile(0, slot, 0) for slot in slots]

    def conds(x, carry):
        here = tiles(V, 0, x + 2)
        for ref, other in (
            (CX.at[x + 1], tiles(V, 0, x + 3)),
            (CZL.at[x], rows_down(here, halo_row(0, 0, x))),
            (CZH.at[x], rows_up(here, halo_row(0, 1, x))),
            (CYL.at[x], lanes_down(here, edges_k[0], x)),
            (CYH.at[x], lanes_up(here, edges_k[1], x)),
        ):
            put(ref, (), tuple((a + b) * 0.5 for a, b in zip(here, other)))
        return carry

    loop(conds, 0)
    ghost_conds()

    def stencil(what, edges, write, carry):
        def body(x, state):
            before, inner = state
            here = tiles(V, what, x + 2)
            after = tuple(c * (n - h) for c, n, h in zip(tiles(CX, x + 1), tiles(V, what, x + 3), here))
            out = tuple(a - b for a, b in zip(before, after))
            for cond, other in (
                (CZL, rows_down(here, halo_row(what, 0, x))),
                (CZH, rows_up(here, halo_row(what, 1, x))),
                (CYL, lanes_down(here, edges[0], x)),
                (CYH, lanes_up(here, edges[1], x)),
            ):
                out = tuple(o + c * (h - n) for o, c, h, n in zip(out, tiles(cond, x), here, other))
            return after, write(x, out, inner)

        first = tuple(c * (n - h) for c, n, h in zip(tiles(CX, 0), tiles(V, what, 2), tiles(V, what, 1)))
        return loop(body, (first, carry))[1]

    def advance(what, edges, depth):
        def write(x, out, packed):
            put(V, (what + 1, x + 2), out)
            return pack_lanes(out, packed, x, 0, depth)

        return stencil(what, edges, write, (blank, blank))

    advance(1, [y_tile(0, slot, 2 * GROUP) for slot in slots], 0)
    edges = ghost_image(0, 1, 2 * GROUP)
    YS[1, 0], YS[1, 1] = advance(2, edges, 2)
    pack_rows(3, 2)
    sent = start_halo(1, 3, 1, 2)
    first_b = send_sum(0, 1, end_sum(0, 0, first_a))
    end_halo(sent, 3, 1, 2)
    advance(3, [y_tile(1, slot, 0) for slot in slots], 0)
    edges = ghost_image(1, 3, 0)
    advance(4, edges, 0)

    moments = end_sum(0, 1, first_b)
    m0, m1, m2 = (full(moments[:, at:at + 1]) for at in range(3))
    c = m1 / m0
    s2 = jnp.maximum(m2 / m0 - c * c, 0.0)

    def basis(x, carry):
        packed, sums = carry
        powers = [tiles(V, at, x + 2) for at in range(1, 6)]
        fields = []
        for half in (0, 1):
            v = [power[half] for power in powers]
            one = [v[at + 1] - c * v[at] for at in range(4)]
            two = [one[at + 1] - c * one[at] - s2 * v[at] for at in range(3)]
            three = [two[at + 1] - c * two[at] - s2 * one[at] for at in range(2)]
            four = three[1] - c * three[0] - s2 * two[0]
            fields.append((v[0], one[0], two[0], three[0], four))
        for at in range(5):
            put(w_ref, (at, x), (fields[0][at], fields[1][at]))
        last = (fields[0][4], fields[1][4])
        put(V, (5, x + 2), last)
        sums = tuple(
            s + fields[0][i] * fields[0][j] + fields[1][i] * fields[1][j] for s, (i, j) in zip(sums, GRAM)
        )
        return pack_lanes(last, packed, x, 0, 1), sums

    packed, sums = loop(basis, ((blank, blank), (blank,) * len(GRAM)))
    second_a = send_sum(1, 0, to_row(sums))
    YS[2, 0], YS[2, 1] = packed
    pack_rows(5, 1)
    sent = start_halo(2, 5, 1, 1)
    end_halo(sent, 5, 1, 1)

    def last_image(x, out, carry):
        put(w_ref, (5, x), out)
        return carry

    stencil(5, [y_tile(2, slot, 0) for slot in slots], last_image, 0)
    second_b = send_sum(1, 1, end_sum(1, 0, second_a))
    entries = end_sum(1, 1, second_b)
    gram = {pair: full(entries[:, at:at + 1]) for at, pair in enumerate(GRAM)}
    at = 0
    for part in solve(gram, c, s2):
        for value in part:
            coef_ref[at] = value
            at += 1

    for copy in everything:
        copy.wait_send()


def combine_kernel(w_ref, coef_ref, solution_ref, residual_ref, image_ref, direction_ref, held, sems):
    refs = (solution_ref, residual_ref, image_ref, direction_ref)
    copies = []
    for part in range(NX // PART):
        for x in range(part * PART, (part + 1) * PART):
            for half in (0, 1):
                at = slice(half * LANES, (half + 1) * LANES)
                w = [w_ref[i, x, half] for i in range(6)]
                start = 0
                for which, count in enumerate((4, 5, 6, 4)):
                    out = coef_ref[start] * w[0]
                    for i in range(1, count):
                        out = out + coef_ref[start + i] * w[i]
                    held[which, x, :, at] = out
                    start += count
        rows = pl.ds(part * PART, PART)
        for which, ref in enumerate(refs):
            copies.append(pltpu.make_async_copy(held.at[which, rows], ref.at[rows], sems.at[which, part]))
            copies[-1].start()
    for copy in copies:
        copy.wait()


def shards(right_side, kappa):
    line, plane = 2 * lax.axis_size("gx"), lax.axis_size("gy") * lax.axis_size("gz") // 2
    hbm = pl.BlockSpec(memory_space=pltpu.MemorySpace.HBM)
    vmem = pl.BlockSpec(memory_space=pltpu.VMEM)
    block, inner = (NX, NZ, NY), (NX, 2, NZ, LANES)
    basis, coefs = pl.pallas_call(
        main_kernel,
        out_shape=(pltpu.VMEM((6,) + inner, F32), pltpu.VMEM((19, NZ, LANES), F32)),
        in_specs=[hbm, hbm],
        out_specs=(vmem, vmem),
        scratch_shapes=[
            pltpu.VMEM((6, NX + 4, 2, NZ, LANES), F32),
            pltpu.VMEM((NX + 1, 2, NZ, LANES), F32),
            pltpu.VMEM(inner, F32),
            pltpu.VMEM(inner, F32),
            pltpu.VMEM(inner, F32),
            pltpu.VMEM(inner, F32),
            pltpu.VMEM((2, 6, 2, NZ, LANES), F32),
            pltpu.VMEM((2, 6, 2, NX, LANES), F32),
            pltpu.VMEM((2, 6, 1, NZ, LANES), F32),
            pltpu.VMEM((6, 2, 2, 2, NX, LANES), F32),
            pltpu.VMEM((6, 2, 2, 2, NX, LANES), F32),
            pltpu.VMEM((3, 2, NZ, LANES), F32),
            pltpu.VMEM((3, 2, NZ, LANES), F32),
            pltpu.VMEM((4, 2, 2, 2, NX, LANES), F32),
            pltpu.VMEM((2, 2, 2, NZ, LANES), F32),
            pltpu.VMEM((2, 2, 2, NZ, LANES), F32),
            pltpu.VMEM((2, 2, 1, LANES), F32),
            pltpu.VMEM((2, line, 1, LANES), F32),
            pltpu.VMEM((2, plane, 1, LANES), F32),
            pltpu.SemaphoreType.DMA((2, 2)),
            pltpu.SemaphoreType.DMA((3, 18)),
            pltpu.SemaphoreType.DMA((3, 18)),
            pltpu.SemaphoreType.DMA((2, 2)),
            pltpu.SemaphoreType.DMA((2, 2)),
        ],
        compiler_params=pltpu.CompilerParams(collective_id=0, has_side_effects=True, vmem_limit_bytes=60 * 2**20),
        name="basis_and_sums",
    )(right_side, kappa)
    return pl.pallas_call(
        combine_kernel,
        out_shape=(jax.ShapeDtypeStruct(block, F32),) * 4,
        in_specs=[vmem, vmem],
        out_specs=(hbm,) * 4,
        scratch_shapes=[pltpu.VMEM((4,) + block, F32), pltpu.SemaphoreType.DMA((4, NX // PART))],
        compiler_params=pltpu.CompilerParams(vmem_limit_bytes=8 * 2**20),
        name="combine",
    )(basis, coefs)


def solution(mesh):
    placed = P("gx", "gz", "gy")
    return jax.shard_map(
        shards,
        mesh=mesh,
        in_specs=(placed, placed),
        out_specs=(placed,) * 4,
        check_vma=False,
    )
```

```python
import functools

import jax
import jax.numpy as jnp
from jax import lax
from jax.experimental import pallas as pl
from jax.experimental.pallas import tpu as pltpu
from jax.sharding import PartitionSpec as P

MESH = pl.DeviceIdType.MESH
F32 = jnp.float32
NX, NZ, NY = 24, 8, 256
LANES = 128
PART = 12
GROUP = 32
FAR = 16
GRAM = ((0, 0), (0, 1), (0, 2), (0, 3), (1, 1), (1, 2), (1, 3), (2, 2), (2, 3), (3, 3), (3, 4))


def shifted(axis, step):
    count = lax.axis_size(axis)
    return {axis: lax.rem(lax.axis_index(axis) + (step + count), count)}


def ring(step, count):
    return min(step % count, (-step) % count)


def group_line():
    lines = lax.axis_size("gx")
    gx, gz = lax.axis_index("gx"), lax.axis_index("gz")
    core = lax.rem(gz, 2)
    offsets = [(d, c) for d in range(lines) for c in range(2) if (d, c) != (0, 0)]
    offsets.sort(key=lambda o: -(2 * ring(o[0], lines) + o[1]))
    peers = [
        (ring(d, lines), {"gx": lax.rem(gx + d, lines), "gz": gz - core + lax.rem(core + c, 2)})
        for d, c in offsets
    ]
    return gx * 2 + core, 2 * lines, peers


def group_plane():
    wide, deep = lax.axis_size("gy"), lax.axis_size("gz") // 2
    gy, gz = lax.axis_index("gy"), lax.axis_index("gz")
    offsets = [(d, e) for d in range(deep) for e in range(wide) if (d, e) != (0, 0)]
    offsets.sort(key=lambda o: -(ring(o[0], deep) + ring(o[1], wide)))
    peers = [
        (ring(d, deep) + ring(e, wide), {"gy": lax.rem(gy + e, wide), "gz": lax.rem(gz + 2 * d, 2 * deep)})
        for d, e in offsets
    ]
    return (gz // 2) * wide + gy, wide * deep, peers


def full(value):
    return jnp.broadcast_to(value, (NZ, LANES))


def total(value):
    return jnp.sum(jnp.sum(value, axis=0, keepdims=True), axis=1, keepdims=True)


def to_row(values):
    lane = lax.broadcasted_iota(jnp.int32, (1, LANES), 1)
    row = jnp.zeros((1, LANES), F32)
    for at, value in enumerate(values):
        row = jnp.where(lane == at, jnp.broadcast_to(total(value), (1, LANES)), row)
    return row


def solve(gram, c, s2):
    zero = jnp.zeros_like(c)
    one = jnp.ones_like(c)

    def g(i, j):
        return gram[(min(i, j), max(i, j))]

    gram = dict(gram)
    gram[(0, 4)] = g(1, 3) - s2 * g(0, 2)
    gram[(1, 4)] = g(2, 3) + s2 * (g(0, 3) - g(1, 2))
    gram[(2, 4)] = g(3, 3) + s2 * (g(1, 3) - g(2, 2))

    def image(a, top):
        out = []
        for i in range(top + 2):
            term = None
            if i <= top:
                term = c * a[i]
            if i >= 1:
                term = a[i - 1] if term is None else term + a[i - 1]
            if i + 1 <= top:
                term = term + s2 * a[i + 1]
            out.append(term)
        return out

    energy = {}
    for i in range(4):
        for j in range(i, 4):
            term = g(i, j + 1) + c * g(i, j)
            if j >= 1:
                term = term + s2 * g(i, j - 1)
            energy[(i, j)] = term

    def form(matrix, a, top):
        out = None
        for i in range(top + 1):
            part = matrix[(i, i)] * a[i]
            for j in range(i + 1, top + 1):
                part = part + (matrix[(i, j)] * 2.0) * a[j]
            out = a[i] * part if out is None else out + a[i] * part
        return out

    rho, way, answer = [one], [], []
    prior_norm = prior_step = None
    for turn in range(4):
        norm_now = form(gram, rho, turn)
        inner = form(energy, rho, turn)
        if turn == 0:
            step = norm_now / inner
            way = list(rho)
        else:
            ratio = norm_now / prior_norm
            step = norm_now / (inner - ratio * norm_now / prior_step)
            way = [rho[i] + ratio * way[i] if i < turn else rho[i] for i in range(turn + 1)]
        answer = [answer[i] + step * way[i] if i < turn else step * way[i] for i in range(turn + 1)]
        moved = image(way, turn)
        rho = [rho[i] - step * moved[i] if i <= turn else zero - step * moved[i] for i in range(turn + 2)]
        prior_norm, prior_step = norm_now, step
    third = image(rho[:4], 3)
    return answer, rho, third + [rho[4]], way


def main_kernel(b_hbm, k_hbm, w_ref, coef_ref,
                V, CX, CZL, CZH, CYL, CYH, GX, GZ, GY, ZS, ZR, YS, YR, XZ, ZY, XY, RS, RA, RB,
                copy_sem, halo_send, halo_recv, red_send, red_recv):
    gx, gy, gz = lax.axis_index("gx"), lax.axis_index("gy"), lax.axis_index("gz")
    core = lax.rem(gz, 2)
    rank_a, count_a, peers_a = group_line()
    rank_b, count_b, peers_b = group_plane()
    across = {"gz": lax.rem(gz + 2 * core - 1 + lax.axis_size("gz"), lax.axis_size("gz"))}
    pairs = (("gx", "gz"), ("gz", "gy"), ("gx", "gy"))
    slots = (0, 1)
    target, inside = {}, {}
    for axis, at in (("gx", gx), ("gy", gy), ("gz", gz)):
        for slot in slots:
            target[(axis, slot)] = shifted(axis, 1 - 2 * slot)
        inside[(axis, 0)], inside[(axis, 1)] = at > 0, at < lax.axis_size(axis) - 1
    corners = [(p, i, q, j) for p, q in pairs for i in slots for j in slots]
    for p, i, q, j in corners:
        target[(p, i, q, j)] = {**target[(p, i)], **target[(q, j)]}
        inside[(p, i, q, j)] = jnp.logical_and(inside[(p, i)], inside[(q, j)])

    barrier = pltpu.get_barrier_semaphore()
    greeted = peers_a + peers_b + [(2, target[corner]) for corner in corners] + [(1, across)]
    greeted.sort(key=lambda pair: -pair[0])

    def greet(some):
        for _, peer in some:
            pl.semaphore_signal(barrier, inc=1, device_id=peer, device_id_type=MESH)

    greet(greeted[:FAR])
    loads = []
    for half in (0, 1):
        at = slice(half * LANES, (half + 1) * LANES)
        for what, ref in ((1, b_hbm), (0, k_hbm)):
            loads.append(pltpu.make_async_copy(ref.at[:, :, at], V.at[what, 2:NX + 2, half], copy_sem.at[what, half]))
    for load in loads:
        load.start()
    greet(greeted[FAR:])

    lane = lax.broadcasted_iota(jnp.int32, (NZ, LANES), 1)
    row = lax.broadcasted_iota(jnp.int32, (NZ, LANES), 0)
    lane_x = lax.broadcasted_iota(jnp.int32, (NX, LANES), 1)
    row_x = lax.broadcasted_iota(jnp.int32, (NX, LANES), 0)
    blank = jnp.zeros((NZ, LANES), F32)
    everything = []

    def faces():
        return [("gz", 0), ("gz", 1)], [("gx", 0), ("gx", 1), ("gy", 0), ("gy", 1)]

    def start_halo(phase, first, count, depth):
        what = pl.ds(first, count)
        ends = {}
        for slot in slots:
            low = NX + 2 - depth if slot == 0 else 2
            ghost = 2 - depth if slot == 0 else NX + 2
            ends[("gx", slot)] = V.at[what, low:low + depth], V.at[what, ghost:ghost + depth]
            ends[("gz", slot)] = ZS.at[what, slot, 0:depth], ZR.at[what, slot, 0:depth]
            ends[("gy", slot)] = YS.at[phase, slot], YR.at[phase, slot]
        for i in slots if depth == 2 else ():
            for j in slots:
                at = NX - 1 if i == 0 else 0
                ends[("gx", i, "gz", j)] = ZS.at[what, j, 0, :, at:at + 1], XZ.at[what, i, j, :, at:at + 1]
                at = NZ - 1 if i == 0 else 0
                ends[("gz", i, "gy", j)] = YS.at[phase, j, at:at + 1], ZY.at[phase, i, j, at:at + 1]
                ends[("gx", i, "gy", j)] = YS.at[phase, j], XY.at[phase, i, j]
        head, tail = faces()
        order = head + (corners if depth == 2 else []) + tail
        sent = []
        for at, name in enumerate(order):
            src, dst = ends[name]
            sent.append(pltpu.make_async_remote_copy(
                src_ref=src, dst_ref=dst, send_sem=halo_send.at[phase, at], recv_sem=halo_recv.at[phase, at],
                device_id=target[name], device_id_type=MESH,
            ))
            sent[-1].start()
        everything.extend(sent)
        return sent

    def keep(flag, value):
        return jnp.where(flag, value, jnp.zeros_like(value))

    def end_halo(sent, first, count, depth):
        for copy in sent:
            copy.wait_recv()
        for what in range(first, first + count):
            for slot in slots:
                for layer in range(depth):
                    at = 1 - layer if slot == 0 else NX + 2 + layer
                    V[what, at] = keep(inside[("gx", slot)], V[what, at])
                    ZR[what, slot, layer] = keep(inside[("gz", slot)], ZR[what, slot, layer])

    def tiles(ref, *at):
        return ref[(*at, 0)], ref[(*at, 1)]

    def put(ref, at, pair):
        ref[(*at, 0)], ref[(*at, 1)] = pair

    def turned(value, by):
        return pltpu.roll(value, by % LANES, 1)

    def lanes_down(pair, packed, x):
        first, second = turned(pair[0], 1), turned(pair[1], 1)
        edge = pltpu.roll(packed, lax.rem(LANES - x, LANES), 1)
        return jnp.where(lane == 0, edge, first), jnp.where(lane == 0, first, second)

    def lanes_up(pair, packed, x):
        first, second = turned(pair[0], -1), turned(pair[1], -1)
        edge = pltpu.roll(packed, LANES - 1 - x, 1)
        return jnp.where(lane == LANES - 1, second, first), jnp.where(lane == LANES - 1, edge, second)

    def rows_down(pair, halo):
        return tuple(jnp.where(row == 0, full(h), pltpu.roll(p, 1, 0)) for p, h in zip(pair, halo))

    def rows_up(pair, halo):
        return tuple(jnp.where(row == NZ - 1, full(h), pltpu.roll(p, NZ - 1, 0)) for p, h in zip(pair, halo))

    def halo_row(what, slot, x):
        return tuple(ZR[what, slot, 0, half, pl.ds(x, 1), :] for half in (0, 1))

    def loop(body, carry):
        return lax.fori_loop(0, NX, body, carry, unroll=True)

    def pack_rows(what, depth):
        flat = V.at[what].reshape((NX + 4) * 2 * NZ, LANES)
        for slot in slots:
            for layer in range(depth):
                at = NZ - 1 - layer if slot == 0 else layer
                for half in (0, 1):
                    ZS[what, slot, layer, half] = flat[pl.ds((4 + half) * NZ + at, NX, stride=2 * NZ), :]

    def pack_lanes(pair, packed, x, start, depth):
        up, down = packed
        for layer in range(depth):
            at = start + GROUP * layer
            here = lane == x + at
            up = jnp.where(here, pltpu.roll(pair[1], lax.rem(x + at + 1 + layer, LANES), 1), up)
            down = jnp.where(here, pltpu.roll(pair[0], lax.rem(x + at + LANES - layer, LANES), 1), down)
        return up, down

    def y_tile(phase, slot, start):
        return turned(keep(inside[("gy", slot)], YR[phase, slot]), -start)

    def ghosts_x(phase, what, start, slot):
        at = 1 if slot == 0 else NX + 2
        x = NX - 1 if slot == 0 else 0
        here = tiles(V, what, at)
        lines = [
            tuple(keep(inside[("gx", slot, "gz", j)], XZ[what, slot, j, half, x:x + 1, :]) for half in (0, 1))
            for j in slots
        ]
        sides = [turned(keep(inside[("gx", slot, "gy", j)], XY[phase, slot, j]), -start) for j in slots]
        return here, (
            tiles(V, what, at - 1), tiles(V, what, at + 1), rows_down(here, lines[0]), rows_up(here, lines[1]),
            lanes_down(here, sides[0], x), lanes_up(here, sides[1], x),
        )

    def ghosts_z(phase, what, start, slot):
        here, outer, inner = tiles(ZR, what, slot, 0), tiles(ZR, what, slot, 1), tiles(ZS, what, 1 - slot, 0)

        def line(i, half):
            at = NX - 1 if i == 0 else 0
            value = keep(inside[("gx", i, "gz", slot)], XZ[what, i, slot, half, at:at + 1, :])
            return jnp.broadcast_to(value, (NX, LANES))

        def column(j):
            at = NZ - 1 if slot == 0 else 0
            value = keep(inside[("gz", slot, "gy", j)], ZY[phase, slot, j, at:at + 1, :])
            spread = jnp.where(lane_x == row_x + start, jnp.broadcast_to(value, (NX, LANES)), 0.0)
            return jnp.broadcast_to(jnp.sum(spread, axis=1, keepdims=True), (NX, LANES))

        before = tuple(jnp.where(row_x == 0, line(0, half), pltpu.roll(here[half], 1, 0)) for half in (0, 1))
        after = tuple(jnp.where(row_x == NX - 1, line(1, half), pltpu.roll(here[half], NX - 1, 0)) for half in (0, 1))
        down = [turned(here[half], 1) for half in (0, 1)]
        up = [turned(here[half], -1) for half in (0, 1)]
        left = jnp.where(lane_x == 0, column(0), down[0]), jnp.where(lane_x == 0, down[0], down[1])
        last = lane_x == LANES - 1
        right = jnp.where(last, up[1], up[0]), jnp.where(last, column(1), up[1])
        return here, (before, after, outer, inner, left, right)

    def ghosts_y(phase, what, start, slot):
        here = y_tile(phase, slot, start)
        outer = y_tile(phase, slot, start + GROUP)
        inner = turned(YS[phase, 1 - slot], -start)
        lines, sides = [], []
        for i in slots:
            at = NZ - 1 if i == 0 else 0
            value = keep(inside[("gz", i, "gy", slot)], ZY[phase, i, slot, at:at + 1, :])
            lines.append(turned(full(value), -start))
            value = turned(keep(inside[("gx", i, "gy", slot)], XY[phase, i, slot]), -start)
            sides.append(turned(value, 1 - NX if i == 0 else NX - 1))
        before = jnp.where(lane == 0, sides[0], turned(here, 1))
        after = jnp.where(lane == NX - 1, sides[1], turned(here, -1))
        low = jnp.where(row == 0, lines[0], pltpu.roll(here, 1, 0))
        high = jnp.where(row == NZ - 1, lines[1], pltpu.roll(here, NZ - 1, 0))
        return (here,), ((before,), (after,), (low,), (high,), (outer,), (inner,))

    regions = ((ghosts_x, GX, "gx"), (ghosts_z, GZ, "gz"), (ghosts_y, GY, "gy"))

    def ghost_conds():
        for find, ref, _ in regions:
            for slot in slots:
                here, others = find(0, 0, 0, slot)
                for at, other in enumerate(others):
                    for part, (a, b) in enumerate(zip(here, other)):
                        ref[slot, at, part] = (a + b) * 0.5

    def ghost_image(phase, what, start):
        sides = []
        for find, ref, axis in regions:
            for slot in slots:
                here, others = find(phase, what, start, slot)
                out = [None] * len(here)
                for at, other in enumerate(others):
                    for part, (a, b) in enumerate(zip(here, other)):
                        term = ref[slot, at, part] * (a - b)
                        out[part] = term if out[part] is None else out[part] + term
                out = tuple(keep(inside[(axis, slot)], value) for value in out)
                if axis == "gx":
                    put(V, (what + 1, 1 if slot == 0 else NX + 2), out)
                elif axis == "gz":
                    put(ZR, (what + 1, slot, 0), out)
                else:
                    sides.append(out[0])
        return sides

    for load in loads:
        load.wait()

    def pack_both(x, packed):
        for what in (0, 1):
            packed = pack_lanes(tiles(V, what, x + 2), packed, x, 2 * GROUP * what, 2)
        return packed

    packed = loop(pack_both, (blank, blank))
    YS[0, 0], YS[0, 1] = packed
    for what in (0, 1):
        pack_rows(what, 2)
    def own_part(x, state):
        before, sums = state
        here, coeff = tiles(V, 1, x + 2), tiles(V, 0, x + 2)
        after = tuple(
            (a + b) * 0.5 * (n - h)
            for a, b, n, h in zip(coeff, tiles(V, 0, x + 3), tiles(V, 1, x + 3), here)
        )
        after = tuple(jnp.where(x < NX - 1, value, 0.0) for value in after)
        out = tuple(a - b for a, b in zip(before, after))
        for shift, edge in ((1, 0), (NZ - 1, NZ - 1)):
            out = tuple(
                o + jnp.where(row == edge, 0.0, (k + pltpu.roll(k, shift, 0)) * 0.5 * (h - pltpu.roll(h, shift, 0)))
                for o, k, h in zip(out, coeff, here)
            )
        for shift, edge, end in ((1, 0, 0), (-1, LANES - 1, 1)):
            k_turn, h_turn = [turned(k, shift) for k in coeff], [turned(h, shift) for h in here]
            terms = []
            for half in (0, 1):
                k_next = k_turn[half] if half == end else jnp.where(lane == edge, k_turn[1 - half], k_turn[half])
                h_next = h_turn[half] if half == end else jnp.where(lane == edge, h_turn[1 - half], h_turn[half])
                term = (coeff[half] + k_next) * 0.5 * (here[half] - h_next)
                terms.append(jnp.where(lane == edge, 0.0, term) if half == end else term)
            out = tuple(o + t for o, t in zip(out, terms))
        sums = (
            sums[0] + here[0] * here[0] + here[1] * here[1],
            sums[1] + here[0] * out[0] + here[1] * out[1],
            sums[2] + out[0] * out[0] + out[1] * out[1],
        )
        return after, sums

    def send_sum(at, which, values):
        rank, count, peers, ref = (
            (rank_a, count_a, peers_a, RA) if which == 0 else (rank_b, count_b, peers_b, RB)
        )
        RS[at, which] = values
        for _, peer in peers:
            pltpu.make_async_remote_copy(
                src_ref=RS.at[at, which], dst_ref=ref.at[at, rank], send_sem=red_send.at[at, which],
                recv_sem=red_recv.at[at, which], device_id=peer, device_id_type=MESH,
            ).start()
        ref[at, rank] = values
        whole = ref.at[at, 0:count - 1]
        waits = pltpu.make_async_remote_copy(
            src_ref=whole, dst_ref=whole, send_sem=red_send.at[at, which], recv_sem=red_recv.at[at, which],
            device_id=peers[0][1], device_id_type=MESH,
        )
        everything.append(waits)
        return waits

    def end_sum(at, which, waits):
        waits.wait_recv()
        return jnp.sum((RA if which == 0 else RB)[at], axis=0)

    sums = to_row(loop(own_part, ((blank, blank), (blank, blank, blank)))[1])
    pl.semaphore_wait(barrier, len(greeted))
    first_a = send_sum(0, 0, sums)
    sent = start_halo(0, 0, 2, 2)
    end_halo(sent, 0, 2, 2)

    put(CX, (0,), tuple((a + b) * 0.5 for a, b in zip(tiles(V, 0, 1), tiles(V, 0, 2))))
    edges_k = [y_tile(0, slot, 0) for slot in slots]

    def conds(x, carry):
        here = tiles(V, 0, x + 2)
        for ref, other in (
            (CX.at[x + 1], tiles(V, 0, x + 3)),
            (CZL.at[x], rows_down(here, halo_row(0, 0, x))),
            (CZH.at[x], rows_up(here, halo_row(0, 1, x))),
            (CYL.at[x], lanes_down(here, edges_k[0], x)),
            (CYH.at[x], lanes_up(here, edges_k[1], x)),
        ):
            put(ref, (), tuple((a + b) * 0.5 for a, b in zip(here, other)))
        return carry

    loop(conds, 0)
    ghost_conds()

    def stencil(what, edges, write, carry):
        def body(x, state):
            before, inner = state
            here = tiles(V, what, x + 2)
            after = tuple(c * (n - h) for c, n, h in zip(tiles(CX, x + 1), tiles(V, what, x + 3), here))
            out = tuple(a - b for a, b in zip(before, after))
            for cond, other in (
                (CZL, rows_down(here, halo_row(what, 0, x))),
                (CZH, rows_up(here, halo_row(what, 1, x))),
                (CYL, lanes_down(here, edges[0], x)),
                (CYH, lanes_up(here, edges[1], x)),
            ):
                out = tuple(o + c * (h - n) for o, c, h, n in zip(out, tiles(cond, x), here, other))
            return after, write(x, out, inner)

        first = tuple(c * (n - h) for c, n, h in zip(tiles(CX, 0), tiles(V, what, 2), tiles(V, what, 1)))
        return loop(body, (first, carry))[1]

    def advance(what, edges, depth):
        def write(x, out, packed):
            put(V, (what + 1, x + 2), out)
            return pack_lanes(out, packed, x, 0, depth)

        return stencil(what, edges, write, (blank, blank))

    advance(1, [y_tile(0, slot, 2 * GROUP) for slot in slots], 0)
    edges = ghost_image(0, 1, 2 * GROUP)
    first_b = send_sum(0, 1, end_sum(0, 0, first_a))
    YS[1, 0], YS[1, 1] = advance(2, edges, 2)
    pack_rows(3, 2)
    sent = start_halo(1, 3, 1, 2)
    end_halo(sent, 3, 1, 2)
    advance(3, [y_tile(1, slot, 0) for slot in slots], 0)
    edges = ghost_image(1, 3, 0)
    advance(4, edges, 0)

    moments = end_sum(0, 1, first_b)
    m0, m1, m2 = (full(moments[:, at:at + 1]) for at in range(3))
    c = m1 / m0
    s2 = jnp.maximum(m2 / m0 - c * c, 0.0)

    def basis(x, carry):
        packed, sums = carry
        powers = [tiles(V, at, x + 2) for at in range(1, 6)]
        fields = []
        for half in (0, 1):
            v = [power[half] for power in powers]
            one = [v[at + 1] - c * v[at] for at in range(4)]
            two = [one[at + 1] - c * one[at] - s2 * v[at] for at in range(3)]
            three = [two[at + 1] - c * two[at] - s2 * one[at] for at in range(2)]
            four = three[1] - c * three[0] - s2 * two[0]
            fields.append((v[0], one[0], two[0], three[0], four))
        for at in range(5):
            put(w_ref, (at, x), (fields[0][at], fields[1][at]))
        last = (fields[0][4], fields[1][4])
        put(V, (5, x + 2), last)
        sums = tuple(
            s + fields[0][i] * fields[0][j] + fields[1][i] * fields[1][j] for s, (i, j) in zip(sums, GRAM)
        )
        return pack_lanes(last, packed, x, 0, 1), sums

    packed, sums = loop(basis, ((blank, blank), (blank,) * len(GRAM)))
    second_a = send_sum(1, 0, to_row(sums))
    YS[2, 0], YS[2, 1] = packed
    pack_rows(5, 1)
    sent = start_halo(2, 5, 1, 1)
    end_halo(sent, 5, 1, 1)

    def last_image(x, out, carry):
        put(w_ref, (5, x), out)
        return carry

    stencil(5, [y_tile(2, slot, 0) for slot in slots], last_image, 0)
    second_b = send_sum(1, 1, end_sum(1, 0, second_a))
    for copy in everything[:-1]:
        copy.wait_send()
    entries = end_sum(1, 1, second_b)
    gram = {pair: full(entries[:, at:at + 1]) for at, pair in enumerate(GRAM)}
    at = 0
    for part in solve(gram, c, s2):
        for value in part:
            coef_ref[at] = value
            at += 1

    second_b.wait_send()


def combine_kernel(w_ref, coef_ref, solution_ref, residual_ref, image_ref, direction_ref, held, sems):
    refs = (solution_ref, residual_ref, image_ref, direction_ref)
    copies = []
    for part in range(NX // PART):
        for x in range(part * PART, (part + 1) * PART):
            for half in (0, 1):
                at = slice(half * LANES, (half + 1) * LANES)
                w = [w_ref[i, x, half] for i in range(6)]
                start = 0
                for which, count in enumerate((4, 5, 6, 4)):
                    out = coef_ref[start] * w[0]
                    for i in range(1, count):
                        out = out + coef_ref[start + i] * w[i]
                    held[which, x, :, at] = out
                    start += count
        rows = pl.ds(part * PART, PART)
        for which, ref in enumerate(refs):
            copies.append(pltpu.make_async_copy(held.at[which, rows], ref.at[rows], sems.at[which, part]))
            copies[-1].start()
    for copy in copies:
        copy.wait()


def shards(right_side, kappa):
    line, plane = 2 * lax.axis_size("gx"), lax.axis_size("gy") * lax.axis_size("gz") // 2
    hbm = pl.BlockSpec(memory_space=pltpu.MemorySpace.HBM)
    vmem = pl.BlockSpec(memory_space=pltpu.VMEM)
    block, inner = (NX, NZ, NY), (NX, 2, NZ, LANES)
    basis, coefs = pl.pallas_call(
        main_kernel,
        out_shape=(pltpu.VMEM((6,) + inner, F32), pltpu.VMEM((19, NZ, LANES), F32)),
        in_specs=[hbm, hbm],
        out_specs=(vmem, vmem),
        scratch_shapes=[
            pltpu.VMEM((6, NX + 4, 2, NZ, LANES), F32),
            pltpu.VMEM((NX + 1, 2, NZ, LANES), F32),
            pltpu.VMEM(inner, F32),
            pltpu.VMEM(inner, F32),
            pltpu.VMEM(inner, F32),
            pltpu.VMEM(inner, F32),
            pltpu.VMEM((2, 6, 2, NZ, LANES), F32),
            pltpu.VMEM((2, 6, 2, NX, LANES), F32),
            pltpu.VMEM((2, 6, 1, NZ, LANES), F32),
            pltpu.VMEM((6, 2, 2, 2, NX, LANES), F32),
            pltpu.VMEM((6, 2, 2, 2, NX, LANES), F32),
            pltpu.VMEM((3, 2, NZ, LANES), F32),
            pltpu.VMEM((3, 2, NZ, LANES), F32),
            pltpu.VMEM((4, 2, 2, 2, NX, LANES), F32),
            pltpu.VMEM((2, 2, 2, NZ, LANES), F32),
            pltpu.VMEM((2, 2, 2, NZ, LANES), F32),
            pltpu.VMEM((2, 2, 1, LANES), F32),
            pltpu.VMEM((2, line, 1, LANES), F32),
            pltpu.VMEM((2, plane, 1, LANES), F32),
            pltpu.SemaphoreType.DMA((2, 2)),
            pltpu.SemaphoreType.DMA((3, 18)),
            pltpu.SemaphoreType.DMA((3, 18)),
            pltpu.SemaphoreType.DMA((2, 2)),
            pltpu.SemaphoreType.DMA((2, 2)),
        ],
        compiler_params=pltpu.CompilerParams(collective_id=0, has_side_effects=True, vmem_limit_bytes=60 * 2**20),
        name="basis_and_sums",
    )(right_side, kappa)
    return pl.pallas_call(
        combine_kernel,
        out_shape=(jax.ShapeDtypeStruct(block, F32),) * 4,
        in_specs=[vmem, vmem],
        out_specs=(hbm,) * 4,
        scratch_shapes=[pltpu.VMEM((4,) + block, F32), pltpu.SemaphoreType.DMA((4, NX // PART))],
        compiler_params=pltpu.CompilerParams(vmem_limit_bytes=8 * 2**20),
        name="combine",
    )(basis, coefs)


def solution(mesh):
    placed = P("gx", "gz", "gy")
    return jax.shard_map(
        shards,
        mesh=mesh,
        in_specs=(placed, placed),
        out_specs=(placed,) * 4,
        check_vma=False,
    )
```

```python
import functools

import jax
import jax.numpy as jnp
from jax import lax
from jax.experimental import pallas as pl
from jax.experimental.pallas import tpu as pltpu
from jax.sharding import PartitionSpec as P

MESH = pl.DeviceIdType.MESH
F32 = jnp.float32
NX, NZ, NY = 24, 8, 256
LANES = 128
PART = 6
GROUP = 32
FAR = 16
GRAM = ((0, 0), (0, 1), (0, 2), (0, 3), (1, 1), (1, 2), (1, 3), (2, 2), (2, 3), (3, 3), (3, 4))


def shifted(axis, step):
    count = lax.axis_size(axis)
    return {axis: lax.rem(lax.axis_index(axis) + (step + count), count)}


def ring(step, count):
    return min(step % count, (-step) % count)


def group_line():
    lines = lax.axis_size("gx")
    gx, gz = lax.axis_index("gx"), lax.axis_index("gz")
    core = lax.rem(gz, 2)
    offsets = [(d, c) for d in range(lines) for c in range(2) if (d, c) != (0, 0)]
    offsets.sort(key=lambda o: -(2 * ring(o[0], lines) + o[1]))
    peers = [
        (ring(d, lines), {"gx": lax.rem(gx + d, lines), "gz": gz - core + lax.rem(core + c, 2)})
        for d, c in offsets
    ]
    return gx * 2 + core, 2 * lines, peers


def group_plane():
    wide, deep = lax.axis_size("gy"), lax.axis_size("gz") // 2
    gy, gz = lax.axis_index("gy"), lax.axis_index("gz")
    offsets = [(d, e) for d in range(deep) for e in range(wide) if (d, e) != (0, 0)]
    offsets.sort(key=lambda o: -(ring(o[0], deep) + ring(o[1], wide)))
    peers = [
        (ring(d, deep) + ring(e, wide), {"gy": lax.rem(gy + e, wide), "gz": lax.rem(gz + 2 * d, 2 * deep)})
        for d, e in offsets
    ]
    return (gz // 2) * wide + gy, wide * deep, peers


def full(value):
    return jnp.broadcast_to(value, (NZ, LANES))


def total(value):
    return jnp.sum(jnp.sum(value, axis=0, keepdims=True), axis=1, keepdims=True)


def to_row(values):
    lane = lax.broadcasted_iota(jnp.int32, (1, LANES), 1)
    row = jnp.zeros((1, LANES), F32)
    for at, value in enumerate(values):
        row = jnp.where(lane == at, jnp.broadcast_to(total(value), (1, LANES)), row)
    return row


def solve(gram, c, s2):
    zero = jnp.zeros_like(c)
    one = jnp.ones_like(c)

    def g(i, j):
        return gram[(min(i, j), max(i, j))]

    gram = dict(gram)
    gram[(0, 4)] = g(1, 3) - s2 * g(0, 2)
    gram[(1, 4)] = g(2, 3) + s2 * (g(0, 3) - g(1, 2))
    gram[(2, 4)] = g(3, 3) + s2 * (g(1, 3) - g(2, 2))

    def image(a, top):
        out = []
        for i in range(top + 2):
            term = None
            if i <= top:
                term = c * a[i]
            if i >= 1:
                term = a[i - 1] if term is None else term + a[i - 1]
            if i + 1 <= top:
                term = term + s2 * a[i + 1]
            out.append(term)
        return out

    energy = {}
    for i in range(4):
        for j in range(i, 4):
            term = g(i, j + 1) + c * g(i, j)
            if j >= 1:
                term = term + s2 * g(i, j - 1)
            energy[(i, j)] = term

    def form(matrix, a, top):
        out = None
        for i in range(top + 1):
            part = matrix[(i, i)] * a[i]
            for j in range(i + 1, top + 1):
                part = part + (matrix[(i, j)] * 2.0) * a[j]
            out = a[i] * part if out is None else out + a[i] * part
        return out

    rho, way, answer = [one], [], []
    prior_norm = prior_step = None
    for turn in range(4):
        norm_now = form(gram, rho, turn)
        inner = form(energy, rho, turn)
        if turn == 0:
            step = norm_now / inner
            way = list(rho)
        else:
            ratio = norm_now / prior_norm
            step = norm_now / (inner - ratio * norm_now / prior_step)
            way = [rho[i] + ratio * way[i] if i < turn else rho[i] for i in range(turn + 1)]
        answer = [answer[i] + step * way[i] if i < turn else step * way[i] for i in range(turn + 1)]
        moved = image(way, turn)
        rho = [rho[i] - step * moved[i] if i <= turn else zero - step * moved[i] for i in range(turn + 2)]
        prior_norm, prior_step = norm_now, step
    third = image(rho[:4], 3)
    return answer, rho, third + [rho[4]], way


def main_kernel(b_hbm, k_hbm, w_ref, coef_ref,
                V, CX, CZL, CZH, CYL, CYH, GX, GZ, GY, ZS, ZR, YS, YR, XZ, ZY, XY, RS, RA, RB,
                copy_sem, halo_send, halo_recv, red_send, red_recv):
    gx, gy, gz = lax.axis_index("gx"), lax.axis_index("gy"), lax.axis_index("gz")
    core = lax.rem(gz, 2)
    rank_a, count_a, peers_a = group_line()
    rank_b, count_b, peers_b = group_plane()
    across = {"gz": lax.rem(gz + 2 * core - 1 + lax.axis_size("gz"), lax.axis_size("gz"))}
    pairs = (("gx", "gz"), ("gz", "gy"), ("gx", "gy"))
    slots = (0, 1)
    target, inside = {}, {}
    for axis, at in (("gx", gx), ("gy", gy), ("gz", gz)):
        for slot in slots:
            target[(axis, slot)] = shifted(axis, 1 - 2 * slot)
        inside[(axis, 0)], inside[(axis, 1)] = at > 0, at < lax.axis_size(axis) - 1
    corners = [(p, i, q, j) for p, q in pairs for i in slots for j in slots]
    for p, i, q, j in corners:
        target[(p, i, q, j)] = {**target[(p, i)], **target[(q, j)]}
        inside[(p, i, q, j)] = jnp.logical_and(inside[(p, i)], inside[(q, j)])

    barrier = pltpu.get_barrier_semaphore()
    greeted = peers_a + peers_b + [(2, target[corner]) for corner in corners] + [(1, across)]
    greeted.sort(key=lambda pair: -pair[0])

    def greet(some):
        for _, peer in some:
            pl.semaphore_signal(barrier, inc=1, device_id=peer, device_id_type=MESH)

    greet(greeted[:FAR])
    loads = []
    for half in (0, 1):
        at = slice(half * LANES, (half + 1) * LANES)
        for what, ref in ((1, b_hbm), (0, k_hbm)):
            loads.append(pltpu.make_async_copy(ref.at[:, :, at], V.at[what, 2:NX + 2, half], copy_sem.at[what, half]))
    for load in loads:
        load.start()
    greet(greeted[FAR:])

    lane = lax.broadcasted_iota(jnp.int32, (NZ, LANES), 1)
    row = lax.broadcasted_iota(jnp.int32, (NZ, LANES), 0)
    lane_x = lax.broadcasted_iota(jnp.int32, (NX, LANES), 1)
    row_x = lax.broadcasted_iota(jnp.int32, (NX, LANES), 0)
    blank = jnp.zeros((NZ, LANES), F32)
    everything = []

    def faces():
        return [("gz", 0), ("gz", 1)], [("gx", 0), ("gx", 1), ("gy", 0), ("gy", 1)]

    def start_halo(phase, first, count, depth):
        what = pl.ds(first, count)
        ends = {}
        for slot in slots:
            low = NX + 2 - depth if slot == 0 else 2
            ghost = 2 - depth if slot == 0 else NX + 2
            ends[("gx", slot)] = V.at[what, low:low + depth], V.at[what, ghost:ghost + depth]
            ends[("gz", slot)] = ZS.at[what, slot, 0:depth], ZR.at[what, slot, 0:depth]
            ends[("gy", slot)] = YS.at[phase, slot], YR.at[phase, slot]
        for i in slots if depth == 2 else ():
            for j in slots:
                at = NX - 1 if i == 0 else 0
                ends[("gx", i, "gz", j)] = ZS.at[what, j, 0, :, at:at + 1], XZ.at[what, i, j, :, at:at + 1]
                at = NZ - 1 if i == 0 else 0
                ends[("gz", i, "gy", j)] = YS.at[phase, j, at:at + 1], ZY.at[phase, i, j, at:at + 1]
                ends[("gx", i, "gy", j)] = YS.at[phase, j], XY.at[phase, i, j]
        head, tail = faces()
        order = head + (corners if depth == 2 else []) + tail
        sent = []
        for at, name in enumerate(order):
            src, dst = ends[name]
            sent.append(pltpu.make_async_remote_copy(
                src_ref=src, dst_ref=dst, send_sem=halo_send.at[phase, at], recv_sem=halo_recv.at[phase, at],
                device_id=target[name], device_id_type=MESH,
            ))
            sent[-1].start()
        everything.extend(sent)
        return sent

    def keep(flag, value):
        return jnp.where(flag, value, jnp.zeros_like(value))

    def end_halo(sent, first, count, depth):
        for copy in sent:
            copy.wait_recv()
        for what in range(first, first + count):
            for slot in slots:
                for layer in range(depth):
                    at = 1 - layer if slot == 0 else NX + 2 + layer
                    V[what, at] = keep(inside[("gx", slot)], V[what, at])
                    ZR[what, slot, layer] = keep(inside[("gz", slot)], ZR[what, slot, layer])

    def tiles(ref, *at):
        return ref[(*at, 0)], ref[(*at, 1)]

    def put(ref, at, pair):
        ref[(*at, 0)], ref[(*at, 1)] = pair

    def turned(value, by):
        return pltpu.roll(value, by % LANES, 1)

    def lanes_down(pair, packed, x):
        first, second = turned(pair[0], 1), turned(pair[1], 1)
        edge = pltpu.roll(packed, lax.rem(LANES - x, LANES), 1)
        return jnp.where(lane == 0, edge, first), jnp.where(lane == 0, first, second)

    def lanes_up(pair, packed, x):
        first, second = turned(pair[0], -1), turned(pair[1], -1)
        edge = pltpu.roll(packed, LANES - 1 - x, 1)
        return jnp.where(lane == LANES - 1, second, first), jnp.where(lane == LANES - 1, edge, second)

    def rows_down(pair, halo):
        return tuple(jnp.where(row == 0, full(h), pltpu.roll(p, 1, 0)) for p, h in zip(pair, halo))

    def rows_up(pair, halo):
        return tuple(jnp.where(row == NZ - 1, full(h), pltpu.roll(p, NZ - 1, 0)) for p, h in zip(pair, halo))

    def halo_row(what, slot, x):
        return tuple(ZR[what, slot, 0, half, pl.ds(x, 1), :] for half in (0, 1))

    def loop(body, carry):
        return lax.fori_loop(0, NX, body, carry, unroll=True)

    def pack_rows(what, depth):
        flat = V.at[what].reshape((NX + 4) * 2 * NZ, LANES)
        for slot in slots:
            for layer in range(depth):
                at = NZ - 1 - layer if slot == 0 else layer
                for half in (0, 1):
                    ZS[what, slot, layer, half] = flat[pl.ds((4 + half) * NZ + at, NX, stride=2 * NZ), :]

    def pack_lanes(pair, packed, x, start, depth):
        up, down = packed
        for layer in range(depth):
            at = start + GROUP * layer
            here = lane == x + at
            up = jnp.where(here, pltpu.roll(pair[1], lax.rem(x + at + 1 + layer, LANES), 1), up)
            down = jnp.where(here, pltpu.roll(pair[0], lax.rem(x + at + LANES - layer, LANES), 1), down)
        return up, down

    def y_tile(phase, slot, start):
        return turned(keep(inside[("gy", slot)], YR[phase, slot]), -start)

    def ghosts_x(phase, what, start, slot):
        at = 1 if slot == 0 else NX + 2
        x = NX - 1 if slot == 0 else 0
        here = tiles(V, what, at)
        lines = [
            tuple(keep(inside[("gx", slot, "gz", j)], XZ[what, slot, j, half, x:x + 1, :]) for half in (0, 1))
            for j in slots
        ]
        sides = [turned(keep(inside[("gx", slot, "gy", j)], XY[phase, slot, j]), -start) for j in slots]
        return here, (
            tiles(V, what, at - 1), tiles(V, what, at + 1), rows_down(here, lines[0]), rows_up(here, lines[1]),
            lanes_down(here, sides[0], x), lanes_up(here, sides[1], x),
        )

    def ghosts_z(phase, what, start, slot):
        here, outer, inner = tiles(ZR, what, slot, 0), tiles(ZR, what, slot, 1), tiles(ZS, what, 1 - slot, 0)

        def line(i, half):
            at = NX - 1 if i == 0 else 0
            value = keep(inside[("gx", i, "gz", slot)], XZ[what, i, slot, half, at:at + 1, :])
            return jnp.broadcast_to(value, (NX, LANES))

        def column(j):
            at = NZ - 1 if slot == 0 else 0
            value = keep(inside[("gz", slot, "gy", j)], ZY[phase, slot, j, at:at + 1, :])
            spread = jnp.where(lane_x == row_x + start, jnp.broadcast_to(value, (NX, LANES)), 0.0)
            return jnp.broadcast_to(jnp.sum(spread, axis=1, keepdims=True), (NX, LANES))

        before = tuple(jnp.where(row_x == 0, line(0, half), pltpu.roll(here[half], 1, 0)) for half in (0, 1))
        after = tuple(jnp.where(row_x == NX - 1, line(1, half), pltpu.roll(here[half], NX - 1, 0)) for half in (0, 1))
        down = [turned(here[half], 1) for half in (0, 1)]
        up = [turned(here[half], -1) for half in (0, 1)]
        left = jnp.where(lane_x == 0, column(0), down[0]), jnp.where(lane_x == 0, down[0], down[1])
        last = lane_x == LANES - 1
        right = jnp.where(last, up[1], up[0]), jnp.where(last, column(1), up[1])
        return here, (before, after, outer, inner, left, right)

    def ghosts_y(phase, what, start, slot):
        here = y_tile(phase, slot, start)
        outer = y_tile(phase, slot, start + GROUP)
        inner = turned(YS[phase, 1 - slot], -start)
        lines, sides = [], []
        for i in slots:
            at = NZ - 1 if i == 0 else 0
            value = keep(inside[("gz", i, "gy", slot)], ZY[phase, i, slot, at:at + 1, :])
            lines.append(turned(full(value), -start))
            value = turned(keep(inside[("gx", i, "gy", slot)], XY[phase, i, slot]), -start)
            sides.append(turned(value, 1 - NX if i == 0 else NX - 1))
        before = jnp.where(lane == 0, sides[0], turned(here, 1))
        after = jnp.where(lane == NX - 1, sides[1], turned(here, -1))
        low = jnp.where(row == 0, lines[0], pltpu.roll(here, 1, 0))
        high = jnp.where(row == NZ - 1, lines[1], pltpu.roll(here, NZ - 1, 0))
        return (here,), ((before,), (after,), (low,), (high,), (outer,), (inner,))

    regions = ((ghosts_x, GX, "gx"), (ghosts_z, GZ, "gz"), (ghosts_y, GY, "gy"))

    def ghost_conds():
        for find, ref, _ in regions:
            found = {}
            for slot in slots:
                here, others = find(0, 0, 0, slot)
                for at, other in enumerate(others):
                    for part, (a, b) in enumerate(zip(here, other)):
                        found[(slot, at, part)] = (a + b) * 0.5
            for name, value in found.items():
                ref[name] = value

    def ghost_image(phase, what, start):
        found, sides = [], []
        for find, ref, axis in regions:
            for slot in slots:
                here, others = find(phase, what, start, slot)
                out = [None] * len(here)
                for at, other in enumerate(others):
                    for part, (a, b) in enumerate(zip(here, other)):
                        term = ref[slot, at, part] * (a - b)
                        out[part] = term if out[part] is None else out[part] + term
                out = tuple(keep(inside[(axis, slot)], value) for value in out)
                if axis == "gx":
                    found.append((V, (what + 1, 1 if slot == 0 else NX + 2), out))
                elif axis == "gz":
                    found.append((ZR, (what + 1, slot, 0), out))
                else:
                    sides.append(out[0])
        for item in found:
            put(*item)
        return sides

    for load in loads:
        load.wait()

    def pack_both(x, packed):
        for what in (0, 1):
            packed = pack_lanes(tiles(V, what, x + 2), packed, x, 2 * GROUP * what, 2)
        return packed

    packed = loop(pack_both, (blank, blank))
    YS[0, 0], YS[0, 1] = packed
    for what in (0, 1):
        pack_rows(what, 2)
    def own_part(x, state):
        before, sums = state
        above = jnp.minimum(x + 3, NX + 1)
        here, coeff = tiles(V, 1, x + 2), tiles(V, 0, x + 2)
        after = tuple(
            (a + b) * 0.5 * (n - h)
            for a, b, n, h in zip(coeff, tiles(V, 0, above), tiles(V, 1, above), here)
        )
        after = tuple(jnp.where(x < NX - 1, value, 0.0) for value in after)
        out = tuple(a - b for a, b in zip(before, after))
        for shift, edge in ((1, 0), (NZ - 1, NZ - 1)):
            out = tuple(
                o + jnp.where(row == edge, 0.0, (k + pltpu.roll(k, shift, 0)) * 0.5 * (h - pltpu.roll(h, shift, 0)))
                for o, k, h in zip(out, coeff, here)
            )
        for shift, edge, end in ((1, 0, 0), (-1, LANES - 1, 1)):
            k_turn, h_turn = [turned(k, shift) for k in coeff], [turned(h, shift) for h in here]
            terms = []
            for half in (0, 1):
                k_next = k_turn[half] if half == end else jnp.where(lane == edge, k_turn[1 - half], k_turn[half])
                h_next = h_turn[half] if half == end else jnp.where(lane == edge, h_turn[1 - half], h_turn[half])
                term = (coeff[half] + k_next) * 0.5 * (here[half] - h_next)
                terms.append(jnp.where(lane == edge, 0.0, term) if half == end else term)
            out = tuple(o + t for o, t in zip(out, terms))
        sums = (
            sums[0] + here[0] * here[0] + here[1] * here[1],
            sums[1] + here[0] * out[0] + here[1] * out[1],
            sums[2] + out[0] * out[0] + out[1] * out[1],
        )
        return after, sums

    def send_sum(at, which, values):
        rank, count, peers, ref = (
            (rank_a, count_a, peers_a, RA) if which == 0 else (rank_b, count_b, peers_b, RB)
        )
        RS[at, which] = values
        for _, peer in peers:
            pltpu.make_async_remote_copy(
                src_ref=RS.at[at, which], dst_ref=ref.at[at, rank], send_sem=red_send.at[at, which],
                recv_sem=red_recv.at[at, which], device_id=peer, device_id_type=MESH,
            ).start()
        ref[at, rank] = values
        whole = ref.at[at, 0:count - 1]
        waits = pltpu.make_async_remote_copy(
            src_ref=whole, dst_ref=whole, send_sem=red_send.at[at, which], recv_sem=red_recv.at[at, which],
            device_id=peers[0][1], device_id_type=MESH,
        )
        everything.append(waits)
        return waits

    def end_sum(at, which, waits):
        waits.wait_recv()
        return jnp.sum((RA if which == 0 else RB)[at], axis=0)

    sums = to_row(loop(own_part, ((blank, blank), (blank, blank, blank)))[1])
    pl.semaphore_wait(barrier, len(greeted))
    first_a = send_sum(0, 0, sums)
    sent = start_halo(0, 0, 2, 2)
    end_halo(sent, 0, 2, 2)

    put(CX, (0,), tuple((a + b) * 0.5 for a, b in zip(tiles(V, 0, 1), tiles(V, 0, 2))))
    edges_k = [y_tile(0, slot, 0) for slot in slots]

    def conds(x, carry):
        here = tiles(V, 0, x + 2)
        for ref, other in (
            (CX.at[x + 1], tiles(V, 0, x + 3)),
            (CZL.at[x], rows_down(here, halo_row(0, 0, x))),
            (CZH.at[x], rows_up(here, halo_row(0, 1, x))),
            (CYL.at[x], lanes_down(here, edges_k[0], x)),
            (CYH.at[x], lanes_up(here, edges_k[1], x)),
        ):
            put(ref, (), tuple((a + b) * 0.5 for a, b in zip(here, other)))
        return carry

    loop(conds, 0)
    ghost_conds()

    def stencil(what, edges, write, carry):
        def body(x, state):
            before, inner = state
            here = tiles(V, what, x + 2)
            after = tuple(c * (n - h) for c, n, h in zip(tiles(CX, x + 1), tiles(V, what, x + 3), here))
            out = tuple(a - b for a, b in zip(before, after))
            for cond, other in (
                (CZL, rows_down(here, halo_row(what, 0, x))),
                (CZH, rows_up(here, halo_row(what, 1, x))),
                (CYL, lanes_down(here, edges[0], x)),
                (CYH, lanes_up(here, edges[1], x)),
            ):
                out = tuple(o + c * (h - n) for o, c, h, n in zip(out, tiles(cond, x), here, other))
            return after, write(x, out, inner)

        first = tuple(c * (n - h) for c, n, h in zip(tiles(CX, 0), tiles(V, what, 2), tiles(V, what, 1)))
        return loop(body, (first, carry))[1]

    def advance(what, edges, depth):
        def write(x, out, packed):
            put(V, (what + 1, x + 2), out)
            return pack_lanes(out, packed, x, 0, depth)

        return stencil(what, edges, write, (blank, blank))

    advance(1, [y_tile(0, slot, 2 * GROUP) for slot in slots], 0)
    edges = ghost_image(0, 1, 2 * GROUP)
    first_b = send_sum(0, 1, end_sum(0, 0, first_a))
    YS[1, 0], YS[1, 1] = advance(2, edges, 2)
    pack_rows(3, 2)
    sent = start_halo(1, 3, 1, 2)
    end_halo(sent, 3, 1, 2)
    advance(3, [y_tile(1, slot, 0) for slot in slots], 0)
    edges = ghost_image(1, 3, 0)
    advance(4, edges, 0)

    moments = end_sum(0, 1, first_b)
    m0, m1, m2 = (full(moments[:, at:at + 1]) for at in range(3))
    c = m1 / m0
    s2 = jnp.maximum(m2 / m0 - c * c, 0.0)

    def basis(x, carry):
        packed, sums = carry
        powers = [tiles(V, at, x + 2) for at in range(1, 6)]
        fields = []
        for half in (0, 1):
            v = [power[half] for power in powers]
            one = [v[at + 1] - c * v[at] for at in range(4)]
            two = [one[at + 1] - c * one[at] - s2 * v[at] for at in range(3)]
            three = [two[at + 1] - c * two[at] - s2 * one[at] for at in range(2)]
            four = three[1] - c * three[0] - s2 * two[0]
            fields.append((v[0], one[0], two[0], three[0], four))
        for at in range(5):
            put(w_ref, (at, x), (fields[0][at], fields[1][at]))
        last = (fields[0][4], fields[1][4])
        put(V, (5, x + 2), last)
        sums = tuple(
            s + fields[0][i] * fields[0][j] + fields[1][i] * fields[1][j] for s, (i, j) in zip(sums, GRAM)
        )
        return pack_lanes(last, packed, x, 0, 1), sums

    packed, sums = loop(basis, ((blank, blank), (blank,) * len(GRAM)))
    second_a = send_sum(1, 0, to_row(sums))
    YS[2, 0], YS[2, 1] = packed
    pack_rows(5, 1)
    sent = start_halo(2, 5, 1, 1)
    end_halo(sent, 5, 1, 1)

    def last_image(x, out, carry):
        put(w_ref, (5, x), out)
        return carry

    stencil(5, [y_tile(2, slot, 0) for slot in slots], last_image, 0)
    second_b = send_sum(1, 1, end_sum(1, 0, second_a))
    for copy in everything[:-1]:
        copy.wait_send()
    entries = end_sum(1, 1, second_b)
    gram = {pair: full(entries[:, at:at + 1]) for at, pair in enumerate(GRAM)}
    at = 0
    for part in solve(gram, c, s2):
        for value in part:
            coef_ref[at] = value
            at += 1

    second_b.wait_send()


def combine_kernel(w_ref, coef_ref, solution_ref, residual_ref, image_ref, direction_ref, held, sems):
    refs = (solution_ref, residual_ref, image_ref, direction_ref)
    copies = []
    for part in range(NX // PART):
        for x in range(part * PART, (part + 1) * PART):
            for half in (0, 1):
                at = slice(half * LANES, (half + 1) * LANES)
                w = [w_ref[i, x, half] for i in range(6)]
                start = 0
                for which, count in enumerate((4, 5, 6, 4)):
                    out = coef_ref[start] * w[0]
                    for i in range(1, count):
                        out = out + coef_ref[start + i] * w[i]
                    held[which, x, :, at] = out
                    start += count
        rows = pl.ds(part * PART, PART)
        for which, ref in enumerate(refs):
            copies.append(pltpu.make_async_copy(held.at[which, rows], ref.at[rows], sems.at[which, part]))
            copies[-1].start()
    for copy in copies:
        copy.wait()


def shards(right_side, kappa):
    line, plane = 2 * lax.axis_size("gx"), lax.axis_size("gy") * lax.axis_size("gz") // 2
    hbm = pl.BlockSpec(memory_space=pltpu.MemorySpace.HBM)
    vmem = pl.BlockSpec(memory_space=pltpu.VMEM)
    block, inner = (NX, NZ, NY), (NX, 2, NZ, LANES)
    basis, coefs = pl.pallas_call(
        main_kernel,
        out_shape=(pltpu.VMEM((6,) + inner, F32), pltpu.VMEM((19, NZ, LANES), F32)),
        in_specs=[hbm, hbm],
        out_specs=(vmem, vmem),
        scratch_shapes=[
            pltpu.VMEM((6, NX + 4, 2, NZ, LANES), F32),
            pltpu.VMEM((NX + 1, 2, NZ, LANES), F32),
            pltpu.VMEM(inner, F32),
            pltpu.VMEM(inner, F32),
            pltpu.VMEM(inner, F32),
            pltpu.VMEM(inner, F32),
            pltpu.VMEM((2, 6, 2, NZ, LANES), F32),
            pltpu.VMEM((2, 6, 2, NX, LANES), F32),
            pltpu.VMEM((2, 6, 1, NZ, LANES), F32),
            pltpu.VMEM((6, 2, 2, 2, NX, LANES), F32),
            pltpu.VMEM((6, 2, 2, 2, NX, LANES), F32),
            pltpu.VMEM((3, 2, NZ, LANES), F32),
            pltpu.VMEM((3, 2, NZ, LANES), F32),
            pltpu.VMEM((4, 2, 2, 2, NX, LANES), F32),
            pltpu.VMEM((2, 2, 2, NZ, LANES), F32),
            pltpu.VMEM((2, 2, 2, NZ, LANES), F32),
            pltpu.VMEM((2, 2, 1, LANES), F32),
            pltpu.VMEM((2, line, 1, LANES), F32),
            pltpu.VMEM((2, plane, 1, LANES), F32),
            pltpu.SemaphoreType.DMA((2, 2)),
            pltpu.SemaphoreType.DMA((3, 18)),
            pltpu.SemaphoreType.DMA((3, 18)),
            pltpu.SemaphoreType.DMA((2, 2)),
            pltpu.SemaphoreType.DMA((2, 2)),
        ],
        compiler_params=pltpu.CompilerParams(collective_id=0, has_side_effects=True, vmem_limit_bytes=60 * 2**20),
        name="basis_and_sums",
    )(right_side, kappa)
    return pl.pallas_call(
        combine_kernel,
        out_shape=(jax.ShapeDtypeStruct(block, F32),) * 4,
        in_specs=[vmem, vmem],
        out_specs=(hbm,) * 4,
        scratch_shapes=[pltpu.VMEM((4,) + block, F32), pltpu.SemaphoreType.DMA((4, NX // PART))],
        compiler_params=pltpu.CompilerParams(vmem_limit_bytes=8 * 2**20),
        name="combine",
    )(basis, coefs)


def solution(mesh):
    placed = P("gx", "gz", "gy")
    return jax.shard_map(
        shards,
        mesh=mesh,
        in_specs=(placed, placed),
        out_specs=(placed,) * 4,
        check_vma=False,
    )
```

```python
import functools

import jax
import jax.numpy as jnp
from jax import lax
from jax.experimental import pallas as pl
from jax.experimental.pallas import tpu as pltpu
from jax.sharding import PartitionSpec as P

MESH = pl.DeviceIdType.MESH
F32 = jnp.float32
NX, NZ, NY = 24, 8, 256
LANES = 128
PART = 6
GROUP = 32
FAR = 16
GRAM = ((0, 0), (0, 1), (0, 2), (0, 3), (1, 1), (1, 2), (1, 3), (2, 2), (2, 3), (3, 3), (3, 4))


def shifted(axis, step):
    count = lax.axis_size(axis)
    return {axis: lax.rem(lax.axis_index(axis) + (step + count), count)}


def ring(step, count):
    return min(step % count, (-step) % count)


def group_line():
    lines = lax.axis_size("gx")
    gx, gz = lax.axis_index("gx"), lax.axis_index("gz")
    core = lax.rem(gz, 2)
    offsets = [(d, c) for d in range(lines) for c in range(2) if (d, c) != (0, 0)]
    offsets.sort(key=lambda o: -(2 * ring(o[0], lines) + o[1]))
    peers = [
        (ring(d, lines), {"gx": lax.rem(gx + d, lines), "gz": gz - core + lax.rem(core + c, 2)})
        for d, c in offsets
    ]
    return gx * 2 + core, 2 * lines, peers


def group_plane():
    wide, deep = lax.axis_size("gy"), lax.axis_size("gz") // 2
    gy, gz = lax.axis_index("gy"), lax.axis_index("gz")
    offsets = [(d, e) for d in range(deep) for e in range(wide) if (d, e) != (0, 0)]
    offsets.sort(key=lambda o: -(ring(o[0], deep) + ring(o[1], wide)))
    peers = [
        (ring(d, deep) + ring(e, wide), {"gy": lax.rem(gy + e, wide), "gz": lax.rem(gz + 2 * d, 2 * deep)})
        for d, e in offsets
    ]
    return (gz // 2) * wide + gy, wide * deep, peers


def full(value):
    return jnp.broadcast_to(value, (NZ, LANES))


def total(value):
    return jnp.sum(jnp.sum(value, axis=0, keepdims=True), axis=1, keepdims=True)


def to_row(values):
    lane = lax.broadcasted_iota(jnp.int32, (1, LANES), 1)
    row = jnp.zeros((1, LANES), F32)
    for at, value in enumerate(values):
        row = jnp.where(lane == at, jnp.broadcast_to(total(value), (1, LANES)), row)
    return row


def solve(gram, c, s2):
    zero = jnp.zeros_like(c)
    one = jnp.ones_like(c)

    def g(i, j):
        return gram[(min(i, j), max(i, j))]

    gram = dict(gram)
    gram[(0, 4)] = g(1, 3) - s2 * g(0, 2)
    gram[(1, 4)] = g(2, 3) + s2 * (g(0, 3) - g(1, 2))
    gram[(2, 4)] = g(3, 3) + s2 * (g(1, 3) - g(2, 2))

    def image(a, top):
        out = []
        for i in range(top + 2):
            term = None
            if i <= top:
                term = c * a[i]
            if i >= 1:
                term = a[i - 1] if term is None else term + a[i - 1]
            if i + 1 <= top:
                term = term + s2 * a[i + 1]
            out.append(term)
        return out

    energy = {}
    for i in range(4):
        for j in range(i, 4):
            term = g(i, j + 1) + c * g(i, j)
            if j >= 1:
                term = term + s2 * g(i, j - 1)
            energy[(i, j)] = term

    def form(matrix, a, top):
        out = None
        for i in range(top + 1):
            part = matrix[(i, i)] * a[i]
            for j in range(i + 1, top + 1):
                part = part + (matrix[(i, j)] * 2.0) * a[j]
            out = a[i] * part if out is None else out + a[i] * part
        return out

    rho, way, answer = [one], [], []
    prior_norm = prior_step = None
    for turn in range(4):
        norm_now = form(gram, rho, turn)
        inner = form(energy, rho, turn)
        if turn == 0:
            step = norm_now / inner
            way = list(rho)
        else:
            ratio = norm_now / prior_norm
            step = norm_now / (inner - ratio * norm_now / prior_step)
            way = [rho[i] + ratio * way[i] if i < turn else rho[i] for i in range(turn + 1)]
        answer = [answer[i] + step * way[i] if i < turn else step * way[i] for i in range(turn + 1)]
        moved = image(way, turn)
        rho = [rho[i] - step * moved[i] if i <= turn else zero - step * moved[i] for i in range(turn + 2)]
        prior_norm, prior_step = norm_now, step
    third = image(rho[:4], 3)
    return answer, rho, third + [rho[4]], way


def main_kernel(b_hbm, k_hbm, w_ref, coef_ref,
                V, CX, CZL, CZH, CYL, CYH, GX, GZ, GY, ZS, ZR, YS, YR, XZ, ZY, XY, RS, RA, RB,
                copy_sem, halo_send, halo_recv, red_send, red_recv):
    gx, gy, gz = lax.axis_index("gx"), lax.axis_index("gy"), lax.axis_index("gz")
    core = lax.rem(gz, 2)
    rank_a, count_a, peers_a = group_line()
    rank_b, count_b, peers_b = group_plane()
    across = {"gz": lax.rem(gz + 2 * core - 1 + lax.axis_size("gz"), lax.axis_size("gz"))}
    pairs = (("gx", "gz"), ("gz", "gy"), ("gx", "gy"))
    slots = (0, 1)
    target, inside = {}, {}
    for axis, at in (("gx", gx), ("gy", gy), ("gz", gz)):
        for slot in slots:
            target[(axis, slot)] = shifted(axis, 1 - 2 * slot)
        inside[(axis, 0)], inside[(axis, 1)] = at > 0, at < lax.axis_size(axis) - 1
    corners = [(p, i, q, j) for p, q in pairs for i in slots for j in slots]
    for p, i, q, j in corners:
        target[(p, i, q, j)] = {**target[(p, i)], **target[(q, j)]}
        inside[(p, i, q, j)] = jnp.logical_and(inside[(p, i)], inside[(q, j)])

    barrier = pltpu.get_barrier_semaphore()
    greeted = peers_a + peers_b + [(2, target[corner]) for corner in corners] + [(1, across)]
    greeted.sort(key=lambda pair: -pair[0])

    def greet(some):
        for _, peer in some:
            pl.semaphore_signal(barrier, inc=1, device_id=peer, device_id_type=MESH)

    greet(greeted[:FAR])
    loads = []
    for half in (0, 1):
        at = slice(half * LANES, (half + 1) * LANES)
        for what, ref in ((1, b_hbm), (0, k_hbm)):
            loads.append(pltpu.make_async_copy(ref.at[:, :, at], V.at[what, 2:NX + 2, half], copy_sem.at[what, half]))
    for load in loads:
        load.start()
    greet(greeted[FAR:])

    lane = lax.broadcasted_iota(jnp.int32, (NZ, LANES), 1)
    row = lax.broadcasted_iota(jnp.int32, (NZ, LANES), 0)
    lane_x = lax.broadcasted_iota(jnp.int32, (NX, LANES), 1)
    row_x = lax.broadcasted_iota(jnp.int32, (NX, LANES), 0)
    blank = jnp.zeros((NZ, LANES), F32)
    everything = []

    def faces():
        return [("gz", 0), ("gz", 1)], [("gx", 0), ("gx", 1), ("gy", 0), ("gy", 1)]

    def start_halo(phase, first, count, depth):
        what = pl.ds(first, count)
        ends = {}
        for slot in slots:
            low = NX + 2 - depth if slot == 0 else 2
            ghost = 2 - depth if slot == 0 else NX + 2
            ends[("gx", slot)] = V.at[what, low:low + depth], V.at[what, ghost:ghost + depth]
            ends[("gz", slot)] = ZS.at[what, slot, 0:depth], ZR.at[what, slot, 0:depth]
            ends[("gy", slot)] = YS.at[phase, slot], YR.at[phase, slot]
        for i in slots if depth == 2 else ():
            for j in slots:
                at = NX - 1 if i == 0 else 0
                ends[("gx", i, "gz", j)] = ZS.at[what, j, 0, :, at:at + 1], XZ.at[what, i, j, :, at:at + 1]
                at = NZ - 1 if i == 0 else 0
                ends[("gz", i, "gy", j)] = YS.at[phase, j, at:at + 1], ZY.at[phase, i, j, at:at + 1]
                ends[("gx", i, "gy", j)] = YS.at[phase, j], XY.at[phase, i, j]
        head, tail = faces()
        order = head + (corners if depth == 2 else []) + tail
        sent = []
        for at, name in enumerate(order):
            src, dst = ends[name]
            sent.append(pltpu.make_async_remote_copy(
                src_ref=src, dst_ref=dst, send_sem=halo_send.at[phase, at], recv_sem=halo_recv.at[phase, at],
                device_id=target[name], device_id_type=MESH,
            ))
            sent[-1].start()
        everything.extend(sent)
        return sent

    def keep(flag, value):
        return jnp.where(flag, value, jnp.zeros_like(value))

    def end_halo(sent, first, count, depth):
        for copy in sent:
            copy.wait_recv()
        for what in range(first, first + count):
            for slot in slots:
                for layer in range(depth):
                    at = 1 - layer if slot == 0 else NX + 2 + layer
                    V[what, at] = keep(inside[("gx", slot)], V[what, at])
                    ZR[what, slot, layer] = keep(inside[("gz", slot)], ZR[what, slot, layer])

    def tiles(ref, *at):
        return ref[(*at, 0)], ref[(*at, 1)]

    def put(ref, at, pair):
        ref[(*at, 0)], ref[(*at, 1)] = pair

    def turned(value, by):
        return pltpu.roll(value, by % LANES, 1)

    def lanes_down(pair, packed, x):
        first, second = turned(pair[0], 1), turned(pair[1], 1)
        edge = pltpu.roll(packed, lax.rem(LANES - x, LANES), 1)
        return jnp.where(lane == 0, edge, first), jnp.where(lane == 0, first, second)

    def lanes_up(pair, packed, x):
        first, second = turned(pair[0], -1), turned(pair[1], -1)
        edge = pltpu.roll(packed, LANES - 1 - x, 1)
        return jnp.where(lane == LANES - 1, second, first), jnp.where(lane == LANES - 1, edge, second)

    def rows_down(pair, halo):
        return tuple(jnp.where(row == 0, full(h), pltpu.roll(p, 1, 0)) for p, h in zip(pair, halo))

    def rows_up(pair, halo):
        return tuple(jnp.where(row == NZ - 1, full(h), pltpu.roll(p, NZ - 1, 0)) for p, h in zip(pair, halo))

    def halo_row(what, slot, x):
        return tuple(ZR[what, slot, 0, half, pl.ds(x, 1), :] for half in (0, 1))

    def loop(body, carry):
        return lax.fori_loop(0, NX, body, carry, unroll=True)

    def pack_rows(what, depth):
        flat = V.at[what].reshape((NX + 4) * 2 * NZ, LANES)
        for slot in slots:
            for layer in range(depth):
                at = NZ - 1 - layer if slot == 0 else layer
                for half in (0, 1):
                    ZS[what, slot, layer, half] = flat[pl.ds((4 + half) * NZ + at, NX, stride=2 * NZ), :]

    def pack_lanes(pair, packed, x, start, depth):
        up, down = packed
        for layer in range(depth):
            at = start + GROUP * layer
            here = lane == x + at
            up = jnp.where(here, pltpu.roll(pair[1], lax.rem(x + at + 1 + layer, LANES), 1), up)
            down = jnp.where(here, pltpu.roll(pair[0], lax.rem(x + at + LANES - layer, LANES), 1), down)
        return up, down

    def y_tile(phase, slot, start):
        return turned(keep(inside[("gy", slot)], YR[phase, slot]), -start)

    def ghosts_x(phase, what, start, slot):
        at = 1 if slot == 0 else NX + 2
        x = NX - 1 if slot == 0 else 0
        here = tiles(V, what, at)
        lines = [
            tuple(keep(inside[("gx", slot, "gz", j)], XZ[what, slot, j, half, x:x + 1, :]) for half in (0, 1))
            for j in slots
        ]
        sides = [turned(keep(inside[("gx", slot, "gy", j)], XY[phase, slot, j]), -start) for j in slots]
        return here, (
            tiles(V, what, at - 1), tiles(V, what, at + 1), rows_down(here, lines[0]), rows_up(here, lines[1]),
            lanes_down(here, sides[0], x), lanes_up(here, sides[1], x),
        )

    def ghosts_z(phase, what, start, slot):
        here, outer, inner = tiles(ZR, what, slot, 0), tiles(ZR, what, slot, 1), tiles(ZS, what, 1 - slot, 0)

        def line(i, half):
            at = NX - 1 if i == 0 else 0
            value = keep(inside[("gx", i, "gz", slot)], XZ[what, i, slot, half, at:at + 1, :])
            return jnp.broadcast_to(value, (NX, LANES))

        def column(j):
            at = NZ - 1 if slot == 0 else 0
            value = keep(inside[("gz", slot, "gy", j)], ZY[phase, slot, j, at:at + 1, :])
            spread = jnp.where(lane_x == row_x + start, jnp.broadcast_to(value, (NX, LANES)), 0.0)
            return jnp.broadcast_to(jnp.sum(spread, axis=1, keepdims=True), (NX, LANES))

        before = tuple(jnp.where(row_x == 0, line(0, half), pltpu.roll(here[half], 1, 0)) for half in (0, 1))
        after = tuple(jnp.where(row_x == NX - 1, line(1, half), pltpu.roll(here[half], NX - 1, 0)) for half in (0, 1))
        down = [turned(here[half], 1) for half in (0, 1)]
        up = [turned(here[half], -1) for half in (0, 1)]
        left = jnp.where(lane_x == 0, column(0), down[0]), jnp.where(lane_x == 0, down[0], down[1])
        last = lane_x == LANES - 1
        right = jnp.where(last, up[1], up[0]), jnp.where(last, column(1), up[1])
        return here, (before, after, outer, inner, left, right)

    def ghosts_y(phase, what, start, slot):
        here = y_tile(phase, slot, start)
        outer = y_tile(phase, slot, start + GROUP)
        inner = turned(YS[phase, 1 - slot], -start)
        lines, sides = [], []
        for i in slots:
            at = NZ - 1 if i == 0 else 0
            value = keep(inside[("gz", i, "gy", slot)], ZY[phase, i, slot, at:at + 1, :])
            lines.append(turned(full(value), -start))
            value = turned(keep(inside[("gx", i, "gy", slot)], XY[phase, i, slot]), -start)
            sides.append(turned(value, 1 - NX if i == 0 else NX - 1))
        before = jnp.where(lane == 0, sides[0], turned(here, 1))
        after = jnp.where(lane == NX - 1, sides[1], turned(here, -1))
        low = jnp.where(row == 0, lines[0], pltpu.roll(here, 1, 0))
        high = jnp.where(row == NZ - 1, lines[1], pltpu.roll(here, NZ - 1, 0))
        return (here,), ((before,), (after,), (low,), (high,), (outer,), (inner,))

    regions = ((ghosts_x, GX, "gx"), (ghosts_z, GZ, "gz"), (ghosts_y, GY, "gy"))

    def ghost_conds():
        for find, ref, _ in regions:
            found = {}
            for slot in slots:
                here, others = find(0, 0, 0, slot)
                for at, other in enumerate(others):
                    for part, (a, b) in enumerate(zip(here, other)):
                        found[(slot, at, part)] = (a + b) * 0.5
            for name, value in found.items():
                ref[name] = value

    def ghost_image(phase, what, start):
        found, sides = [], []
        for find, ref, axis in regions:
            for slot in slots:
                here, others = find(phase, what, start, slot)
                out = [None] * len(here)
                for at, other in enumerate(others):
                    for part, (a, b) in enumerate(zip(here, other)):
                        term = ref[slot, at, part] * (a - b)
                        out[part] = term if out[part] is None else out[part] + term
                out = tuple(keep(inside[(axis, slot)], value) for value in out)
                if axis == "gx":
                    found.append((V, (what + 1, 1 if slot == 0 else NX + 2), out))
                elif axis == "gz":
                    found.append((ZR, (what + 1, slot, 0), out))
                else:
                    sides.append(out[0])
        for item in found:
            put(*item)
        return sides

    for load in loads:
        load.wait()

    def pack_both(x, packed):
        for what in (0, 1):
            packed = pack_lanes(tiles(V, what, x + 2), packed, x, 2 * GROUP * what, 2)
        return packed

    packed = loop(pack_both, (blank, blank))
    YS[0, 0], YS[0, 1] = packed
    for what in (0, 1):
        pack_rows(what, 2)
    def own_part(x, state):
        before, sums = state
        above = jnp.minimum(x + 3, NX + 1)
        here, coeff = tiles(V, 1, x + 2), tiles(V, 0, x + 2)
        after = tuple(
            (a + b) * 0.5 * (n - h)
            for a, b, n, h in zip(coeff, tiles(V, 0, above), tiles(V, 1, above), here)
        )
        after = tuple(jnp.where(x < NX - 1, value, 0.0) for value in after)
        out = tuple(a - b for a, b in zip(before, after))
        for shift, edge in ((1, 0), (NZ - 1, NZ - 1)):
            out = tuple(
                o + jnp.where(row == edge, 0.0, (k + pltpu.roll(k, shift, 0)) * 0.5 * (h - pltpu.roll(h, shift, 0)))
                for o, k, h in zip(out, coeff, here)
            )
        for shift, edge, end in ((1, 0, 0), (-1, LANES - 1, 1)):
            k_turn, h_turn = [turned(k, shift) for k in coeff], [turned(h, shift) for h in here]
            terms = []
            for half in (0, 1):
                k_next = k_turn[half] if half == end else jnp.where(lane == edge, k_turn[1 - half], k_turn[half])
                h_next = h_turn[half] if half == end else jnp.where(lane == edge, h_turn[1 - half], h_turn[half])
                term = (coeff[half] + k_next) * 0.5 * (here[half] - h_next)
                terms.append(jnp.where(lane == edge, 0.0, term) if half == end else term)
            out = tuple(o + t for o, t in zip(out, terms))
        sums = (
            sums[0] + here[0] * here[0] + here[1] * here[1],
            sums[1] + here[0] * out[0] + here[1] * out[1],
            sums[2] + out[0] * out[0] + out[1] * out[1],
        )
        return after, sums

    def send_sum(at, which, values):
        rank, count, peers, ref = (
            (rank_a, count_a, peers_a, RA) if which == 0 else (rank_b, count_b, peers_b, RB)
        )
        RS[at, which] = values
        for _, peer in peers:
            pltpu.make_async_remote_copy(
                src_ref=RS.at[at, which], dst_ref=ref.at[at, rank], send_sem=red_send.at[at, which],
                recv_sem=red_recv.at[at, which], device_id=peer, device_id_type=MESH,
            ).start()
        ref[at, rank] = values
        whole = ref.at[at, 0:count - 1]
        waits = pltpu.make_async_remote_copy(
            src_ref=whole, dst_ref=whole, send_sem=red_send.at[at, which], recv_sem=red_recv.at[at, which],
            device_id=peers[0][1], device_id_type=MESH,
        )
        everything.append(waits)
        return waits

    def end_sum(at, which, waits):
        waits.wait_recv()
        return jnp.sum((RA if which == 0 else RB)[at], axis=0)

    sums = to_row(loop(own_part, ((blank, blank), (blank, blank, blank)))[1])
    pl.semaphore_wait(barrier, len(greeted))
    first_a = send_sum(0, 0, sums)
    sent = start_halo(0, 0, 2, 2)
    end_halo(sent, 0, 2, 2)

    put(CX, (0,), tuple((a + b) * 0.5 for a, b in zip(tiles(V, 0, 1), tiles(V, 0, 2))))
    edges_k = [y_tile(0, slot, 0) for slot in slots]

    def conds(x, carry):
        here = tiles(V, 0, x + 2)
        for ref, other in (
            (CX.at[x + 1], tiles(V, 0, x + 3)),
            (CZL.at[x], rows_down(here, halo_row(0, 0, x))),
            (CZH.at[x], rows_up(here, halo_row(0, 1, x))),
            (CYL.at[x], lanes_down(here, edges_k[0], x)),
            (CYH.at[x], lanes_up(here, edges_k[1], x)),
        ):
            put(ref, (), tuple((a + b) * 0.5 for a, b in zip(here, other)))
        return carry

    loop(conds, 0)
    ghost_conds()

    def stencil(what, edges, write, carry):
        def body(x, state):
            before, inner = state
            here = tiles(V, what, x + 2)
            after = tuple(c * (n - h) for c, n, h in zip(tiles(CX, x + 1), tiles(V, what, x + 3), here))
            out = tuple(a - b for a, b in zip(before, after))
            for cond, other in (
                (CZL, rows_down(here, halo_row(what, 0, x))),
                (CZH, rows_up(here, halo_row(what, 1, x))),
                (CYL, lanes_down(here, edges[0], x)),
                (CYH, lanes_up(here, edges[1], x)),
            ):
                out = tuple(o + c * (h - n) for o, c, h, n in zip(out, tiles(cond, x), here, other))
            return after, write(x, out, inner)

        first = tuple(c * (n - h) for c, n, h in zip(tiles(CX, 0), tiles(V, what, 2), tiles(V, what, 1)))
        return loop(body, (first, carry))[1]

    def advance(what, edges, depth):
        def write(x, out, packed):
            put(V, (what + 1, x + 2), out)
            return pack_lanes(out, packed, x, 0, depth)

        return stencil(what, edges, write, (blank, blank))

    advance(1, [y_tile(0, slot, 2 * GROUP) for slot in slots], 0)
    edges = ghost_image(0, 1, 2 * GROUP)
    first_b = send_sum(0, 1, end_sum(0, 0, first_a))
    YS[1, 0], YS[1, 1] = advance(2, edges, 2)
    pack_rows(3, 2)
    sent = start_halo(1, 3, 1, 2)
    end_halo(sent, 3, 1, 2)
    advance(3, [y_tile(1, slot, 0) for slot in slots], 0)
    edges = ghost_image(1, 3, 0)
    advance(4, edges, 0)

    moments = end_sum(0, 1, first_b)
    m0, m1, m2 = (full(moments[:, at:at + 1]) for at in range(3))
    c = m1 / m0
    s2 = jnp.maximum(m2 / m0 - c * c, 0.0)

    def basis(x):
        powers = [tiles(V, at, x + 2) for at in range(1, 6)]
        fields = []
        for half in (0, 1):
            v = [power[half] for power in powers]
            one = [v[at + 1] - c * v[at] for at in range(4)]
            two = [one[at + 1] - c * one[at] - s2 * v[at] for at in range(3)]
            three = [two[at + 1] - c * two[at] - s2 * one[at] for at in range(2)]
            four = three[1] - c * three[0] - s2 * two[0]
            fields.append((v[0], one[0], two[0], three[0], four))
        return fields

    def products(x, sums):
        low, high = basis(x)
        return tuple(s + low[i] * low[j] + high[i] * high[j] for s, (i, j) in zip(sums, GRAM))

    def keep_basis(x, packed):
        low, high = basis(x)
        for at in range(5):
            put(w_ref, (at, x), (low[at], high[at]))
        last = (low[4], high[4])
        put(V, (5, x + 2), last)
        return pack_lanes(last, packed, x, 0, 1)

    second_a = send_sum(1, 0, to_row(loop(products, (blank,) * len(GRAM))))
    YS[2, 0], YS[2, 1] = loop(keep_basis, (blank, blank))
    pack_rows(5, 1)
    sent = start_halo(2, 5, 1, 1)
    end_halo(sent, 5, 1, 1)

    def last_image(x, out, carry):
        put(w_ref, (5, x), out)
        return carry

    stencil(5, [y_tile(2, slot, 0) for slot in slots], last_image, 0)
    second_b = send_sum(1, 1, end_sum(1, 0, second_a))
    for copy in everything[:-1]:
        copy.wait_send()
    entries = end_sum(1, 1, second_b)
    gram = {pair: full(entries[:, at:at + 1]) for at, pair in enumerate(GRAM)}
    at = 0
    for part in solve(gram, c, s2):
        for value in part:
            coef_ref[at] = value
            at += 1

    second_b.wait_send()


def combine_kernel(w_ref, coef_ref, solution_ref, residual_ref, image_ref, direction_ref, held, sems):
    refs = (solution_ref, residual_ref, image_ref, direction_ref)
    copies = []
    for part in range(NX // PART):
        for x in range(part * PART, (part + 1) * PART):
            for half in (0, 1):
                at = slice(half * LANES, (half + 1) * LANES)
                w = [w_ref[i, x, half] for i in range(6)]
                start = 0
                for which, count in enumerate((4, 5, 6, 4)):
                    out = coef_ref[start] * w[0]
                    for i in range(1, count):
                        out = out + coef_ref[start + i] * w[i]
                    held[which, x, :, at] = out
                    start += count
        rows = pl.ds(part * PART, PART)
        for which, ref in enumerate(refs):
            copies.append(pltpu.make_async_copy(held.at[which, rows], ref.at[rows], sems.at[which, part]))
            copies[-1].start()
    for copy in copies:
        copy.wait()


def shards(right_side, kappa):
    line, plane = 2 * lax.axis_size("gx"), lax.axis_size("gy") * lax.axis_size("gz") // 2
    hbm = pl.BlockSpec(memory_space=pltpu.MemorySpace.HBM)
    vmem = pl.BlockSpec(memory_space=pltpu.VMEM)
    block, inner = (NX, NZ, NY), (NX, 2, NZ, LANES)
    basis, coefs = pl.pallas_call(
        main_kernel,
        out_shape=(pltpu.VMEM((6,) + inner, F32), pltpu.VMEM((19, NZ, LANES), F32)),
        in_specs=[hbm, hbm],
        out_specs=(vmem, vmem),
        scratch_shapes=[
            pltpu.VMEM((6, NX + 4, 2, NZ, LANES), F32),
            pltpu.VMEM((NX + 1, 2, NZ, LANES), F32),
            pltpu.VMEM(inner, F32),
            pltpu.VMEM(inner, F32),
            pltpu.VMEM(inner, F32),
            pltpu.VMEM(inner, F32),
            pltpu.VMEM((2, 6, 2, NZ, LANES), F32),
            pltpu.VMEM((2, 6, 2, NX, LANES), F32),
            pltpu.VMEM((2, 6, 1, NZ, LANES), F32),
            pltpu.VMEM((6, 2, 2, 2, NX, LANES), F32),
            pltpu.VMEM((6, 2, 2, 2, NX, LANES), F32),
            pltpu.VMEM((3, 2, NZ, LANES), F32),
            pltpu.VMEM((3, 2, NZ, LANES), F32),
            pltpu.VMEM((4, 2, 2, 2, NX, LANES), F32),
            pltpu.VMEM((2, 2, 2, NZ, LANES), F32),
            pltpu.VMEM((2, 2, 2, NZ, LANES), F32),
            pltpu.VMEM((2, 2, 1, LANES), F32),
            pltpu.VMEM((2, line, 1, LANES), F32),
            pltpu.VMEM((2, plane, 1, LANES), F32),
            pltpu.SemaphoreType.DMA((2, 2)),
            pltpu.SemaphoreType.DMA((3, 18)),
            pltpu.SemaphoreType.DMA((3, 18)),
            pltpu.SemaphoreType.DMA((2, 2)),
            pltpu.SemaphoreType.DMA((2, 2)),
        ],
        compiler_params=pltpu.CompilerParams(collective_id=0, has_side_effects=True, vmem_limit_bytes=60 * 2**20),
        name="basis_and_sums",
    )(right_side, kappa)
    return pl.pallas_call(
        combine_kernel,
        out_shape=(jax.ShapeDtypeStruct(block, F32),) * 4,
        in_specs=[vmem, vmem],
        out_specs=(hbm,) * 4,
        scratch_shapes=[pltpu.VMEM((4,) + block, F32), pltpu.SemaphoreType.DMA((4, NX // PART))],
        compiler_params=pltpu.CompilerParams(vmem_limit_bytes=8 * 2**20),
        name="combine",
    )(basis, coefs)


def solution(mesh):
    placed = P("gx", "gz", "gy")
    return jax.shard_map(
        shards,
        mesh=mesh,
        in_specs=(placed, placed),
        out_specs=(placed,) * 4,
        check_vma=False,
    )
```
